256 devices in a mesh: slab: 16 (over x, y), cross: 16 (over z, core).
Axes of the slice: x: 4, y: 4, z: 8, core: 2. Of those that a mesh axis runs over, the one named last changes fastest.
Arguments:
- rhs: bfloat16 [16, 16, 32, 128, 128], P('slab', 'cross'), may hold values from -6 to 6
- m_blocks: bfloat16 [16, 16, 72, 3, 128, 128], P('slab', 'cross'), may hold values from -0.3125 to 0.3125
- m_cols: int32 [16, 16, 72, 3], P('slab', 'cross'), may hold values from 0 to 71, as said below
- j_blocks: bfloat16 [16, 16, 32, 3, 128, 128], P('slab', 'cross'), may hold values from -0.3125 to 0.3125
- j_cols: int32 [16, 16, 32, 3], P('slab', 'cross'), may hold values from 0 to 71, as said below
- send_list: int32 [16, 16, 16, 2], P('slab', 'cross'), may hold values from 0 to 31, as said below
- send_count: int32 [16, 16, 16], P('slab', 'cross'), may hold values from 0 to 2, as said below
Outputs:
- second_iterate: bfloat16 [16, 16, 32, 128, 128], P('slab', 'cross')
The draws below stay inside these ranges and needn't reach their ends.
Inputs may be any that keep to these rules, and one draw needn't show every extreme that they name: `m_cols`: each row's first block column is the row itself; the others differ from it and from each other. `j_cols`: each row's first block column is the row itself; the others differ from it and from each other. `send_list`: the used slots of one list name different block rows. `send_count`: no subdomain lends rows to itself; in every slab index some subdomain receives 2 rows from each other one.
All inputs are finite; a program needn't handle non-finite values.
Results may differ from the reference program's by a relative error of at most 0.0058.
Values may be sent and summed in bfloat16 or wider, within the bound.
No kernel may reach another device: no remote copies, remote signals or barrier semaphores. Data moves between devices by JAX's collectives and lax.ppermute only.
A program may use at most 64 MiB of HBM per device.

```python
import jax
import jax.numpy as jnp
from jax import lax

BLK = 128
NV = 128
ROWS = 32
OVL = 4
CAP = 2
NBLK = 3
EXT = 72
N_SLAB = 16
N_CROSS = 16


def pattern_cols(key, row_total, span):
    leading = (N_SLAB, N_CROSS, row_total)
    row_ids = jnp.arange(row_total, dtype=jnp.int32)
    columns = [jnp.broadcast_to(row_ids, leading)]
    for slot_num in range(1, NBLK):
        lower_end = 1 + (slot_num - 1) * (span - 1) // (NBLK - 1)
        upper_end = 1 + slot_num * (span - 1) // (NBLK - 1)
        offset = jax.random.randint(jax.random.fold_in(key, slot_num), leading, lower_end, upper_end, dtype=jnp.int32)
        columns.append((row_ids + offset) % span)
    return jnp.stack(columns, axis=-1)


def draw_m_cols(key, part):
    return pattern_cols(jax.random.fold_in(key, 11), EXT, EXT)


def draw_j_cols(key, part):
    columns = pattern_cols(jax.random.fold_in(key, 23), ROWS, EXT)
    return columns.at[0, 0, 0, NBLK - 1].set(EXT - 1)


def draw_send_count(key, part):
    counts = jax.random.randint(jax.random.fold_in(key, 31), (N_SLAB, N_CROSS, N_CROSS), 0, CAP + 1, dtype=jnp.int32)
    chosen = jax.random.randint(jax.random.fold_in(key, 37), (N_SLAB,), 0, N_CROSS, dtype=jnp.int32)
    peer_ids = jnp.arange(N_CROSS, dtype=jnp.int32)
    filled = peer_ids[None, None, :] == chosen[:, None, None]
    counts = jnp.where(filled, CAP, counts)
    itself = peer_ids[None, :, None] == peer_ids[None, None, :]
    return jnp.where(itself, 0, counts).astype(jnp.int32)


def draw_send_list(key, part):
    starts = jax.random.randint(jax.random.fold_in(key, 41), (N_SLAB, N_CROSS, N_CROSS), 0, ROWS, dtype=jnp.int32)
    starts = starts.at[0, 0, 0].set(ROWS - 1).at[0, 0, 1].set(0)
    slots = [starts]
    for slot_num in range(1, CAP):
        lower_end = slot_num * ROWS // CAP
        upper_end = (slot_num + 1) * ROWS // CAP
        offset = jax.random.randint(jax.random.fold_in(key, 50 + slot_num), (N_SLAB, N_CROSS, N_CROSS), lower_end, upper_end, dtype=jnp.int32)
        slots.append((starts + offset) % ROWS)
    return jnp.stack(slots, axis=-1).astype(jnp.int32)


def level_of(key, dims, shards, low, top_value):
    level, own = 1.0, jax.random.fold_in(key, 6)
    for position, parts in shards:
        steps = jnp.exp(jax.random.uniform(jax.random.fold_in(own, position), (parts,), jnp.float32, low / len(shards), top_value / len(shards)))
        level = level * jnp.repeat(steps, dims[position] // parts).reshape([-1 if axis == position else 1 for axis in range(len(dims))])
    return level


def noise(rng, shape, scale, limit, split=(), kind=jnp.bfloat16):
    loudness = level_of(rng, shape, split, -0.22, 0.18) if split else 1.0
    values = jax.random.normal(rng, shape, jnp.float32) * scale * loudness
    return jnp.minimum(jnp.maximum(values, -limit), limit).astype(kind)


def setup_inputs(seed: int = 0) -> dict:
    streams_of = jax.random.split(jax.random.key(seed), 8)
    return {
        "rhs": noise(streams_of[0], (N_SLAB, N_CROSS, ROWS, BLK, NV), 1.0, 6.0, ((0, 16), (1, 16))),
        "m_blocks": noise(streams_of[1], (N_SLAB, N_CROSS, EXT, NBLK, BLK, BLK), (NBLK * BLK) ** -0.5, 0.3125, ((0, 16), (1, 16))),
        "m_cols": draw_m_cols(jax.random.fold_in(streams_of[7], 71), 0),
        "j_blocks": noise(streams_of[3], (N_SLAB, N_CROSS, ROWS, NBLK, BLK, BLK), (NBLK * BLK) ** -0.5, 0.3125, ((0, 16), (1, 16))),
        "j_cols": draw_j_cols(jax.random.fold_in(streams_of[7], 71), 0),
        "send_list": draw_send_list(jax.random.fold_in(streams_of[7], 71), 0),
        "send_count": draw_send_count(jax.random.fold_in(streams_of[7], 71), 0),
    }


def extend_all(field, send_list, send_count):
    zeros = jnp.zeros_like(field[:1, :, :OVL])
    upper = jnp.concatenate([zeros, field[:-1, :, ROWS - OVL:]], axis=0)
    lower = jnp.concatenate([field[1:, :, :OVL], zeros], axis=0)
    picked = jax.vmap(jax.vmap(lambda source_rows, picks: jnp.take(source_rows, picks.reshape(-1), axis=0)))(field, send_list)
    picked = picked.reshape(N_SLAB, N_CROSS, N_CROSS, CAP, BLK, NV)
    valid = jnp.arange(CAP, dtype=jnp.int32)[None, None, None, :] < send_count[..., None]
    picked = jnp.where(valid[..., None, None], picked, jnp.zeros((), field.dtype))
    arrived = jnp.swapaxes(picked, 1, 2).reshape(N_SLAB, N_CROSS, N_CROSS * CAP, BLK, NV)
    return jnp.concatenate([field, upper, lower, arrived], axis=2)


def apply_blocks(blocks, columns, extended):
    flat_blocks = blocks.reshape((N_SLAB * N_CROSS,) + blocks.shape[2:])
    flat_cols = columns.reshape((N_SLAB * N_CROSS,) + columns.shape[2:])
    flat_ext = extended.reshape((N_SLAB * N_CROSS,) + extended.shape[2:])

    def single(items):
        block_set, col_set, ext_set = items
        gathered = jnp.take(ext_set, col_set, axis=0).astype(jnp.float32)
        return jnp.einsum('ekab,ekbn->ean', block_set.astype(jnp.float32), gathered)

    result = lax.map(single, (flat_blocks, flat_cols, flat_ext))
    return result.reshape((N_SLAB, N_CROSS) + result.shape[1:])


def assemble(partial_value, send_list, send_count):
    total = partial_value[:, :, :ROWS].astype(jnp.float32)
    upper_part = partial_value[:, :, ROWS:ROWS + OVL]
    lower_part = partial_value[:, :, ROWS + OVL:ROWS + 2 * OVL]
    zeros = jnp.zeros_like(upper_part[:1])
    from_prev = jnp.concatenate([zeros, lower_part[:-1]], axis=0).astype(jnp.float32)
    from_next = jnp.concatenate([upper_part[1:], zeros], axis=0).astype(jnp.float32)
    total = total.at[:, :, :OVL].add(from_prev)
    total = total.at[:, :, ROWS - OVL:].add(from_next)
    cross_part = partial_value[:, :, ROWS + 2 * OVL:].reshape(N_SLAB, N_CROSS, N_CROSS, CAP, BLK * NV)
    returned = jnp.swapaxes(cross_part, 1, 2).reshape(N_SLAB, N_CROSS, N_CROSS * CAP, BLK * NV).astype(jnp.float32)
    valid = (jnp.arange(CAP, dtype=jnp.int32)[None, None, None, :] < send_count[..., None]).reshape(N_SLAB, N_CROSS, N_CROSS * CAP)
    targets = send_list.reshape(N_SLAB, N_CROSS, N_CROSS * CAP)
    table = ((targets[:, :, None, :] == jnp.arange(ROWS, dtype=jnp.int32)[None, None, :, None]) & valid[:, :, None, :]).astype(jnp.float32)
    added = jnp.einsum('scrj,scjm->scrm', table, returned, precision=lax.Precision.HIGHEST)
    return total + added.reshape(N_SLAB, N_CROSS, ROWS, BLK, NV)


def precondition(field, m_blocks, m_cols, send_list, send_count):
    extended = extend_all(field, send_list, send_count)
    partial_value = apply_blocks(m_blocks, m_cols, extended).astype(jnp.bfloat16)
    return assemble(partial_value, send_list, send_count)


def reference(rhs, m_blocks, m_cols, j_blocks, j_cols, send_list, send_count):
    first = precondition(rhs, m_blocks, m_cols, send_list, send_count).astype(jnp.bfloat16)
    extended = extend_all(first, send_list, send_count)
    image = apply_blocks(j_blocks, j_cols, extended)
    residual = (rhs.astype(jnp.float32) - image).astype(jnp.bfloat16)
    second = first.astype(jnp.float32) + precondition(residual, m_blocks, m_cols, send_list, send_count)
    return second.astype(jnp.bfloat16)
```

```python
import functools

import jax
import jax.numpy as jnp
from jax import lax
from jax.experimental import pallas as pl
from jax.experimental.pallas import tpu as pltpu
from jax.sharding import PartitionSpec as P

OVL = 4
BF = jnp.bfloat16
F32 = jnp.float32
VM = pl.BlockSpec(memory_space=pltpu.VMEM)
SM = pl.BlockSpec(memory_space=pltpu.SMEM)
HB = pl.BlockSpec(memory_space=pl.ANY)


def in_vmem(x):
    return pltpu.with_memory_space_constraint(x, pltpu.VMEM)


def params():
    return pltpu.CompilerParams(vmem_limit_bytes=12 * 1024 * 1024)


def cost(flops, nbytes):
    return pl.CostEstimate(flops=flops, bytes_accessed=nbytes, transcendentals=0)


def slot_target(list_ref, count_ref, slot, slots):
    peer, turn = slot // slots, slot % slots
    return list_ref[0, 0, peer, turn], turn < count_ref[0, 0, peer]


def pack_rows(field_ref, list_ref, count_ref, out_ref, slots):
    for slot in range(out_ref.shape[0] * slots):
        row, used = slot_target(list_ref, count_ref, slot, slots)
        out_ref[slot // slots, slot % slots] = jnp.where(used, field_ref[row], jnp.zeros((), BF))


def pack_rhs_kernel(list_ref, count_ref, rhs_ref, out_ref, head_ref, tail_ref):
    rows = rhs_ref.shape[2]
    field = rhs_ref.at[0, 0]
    pack_rows(field, list_ref, count_ref, out_ref, out_ref.shape[1])
    head_ref[...] = field[:OVL]
    tail_ref[...] = field[rows - OVL :]


def fill_extended(ext_ref, own, upper_ref, lower_ref, incoming_ref):
    rows = own.shape[0]
    ext_ref[:rows] = own[...]
    ext_ref[rows : rows + OVL] = upper_ref[...]
    ext_ref[rows + OVL : rows + 2 * OVL] = lower_ref[...]
    peers, slots = incoming_ref.shape[:2]
    for peer in range(peers):
        base = rows + 2 * OVL + peer * slots
        ext_ref[base : base + slots] = incoming_ref[peer]


def row_product(blocks_ref, cols_ref, ext_ref, row):
    terms = blocks_ref.shape[3]
    left = jnp.concatenate([blocks_ref[0, 0, row, k] for k in range(terms)], axis=1)
    right = jnp.concatenate([ext_ref[cols_ref[0, 0, row, k]] for k in range(terms)], axis=0)
    return jnp.dot(left, right, preferred_element_type=F32)


def margin_kernel(cols_ref, own_ref, upper_ref, lower_ref, incoming_ref, blocks_ref, prev_ref, next_ref, cross_ref, ext_ref):
    own = own_ref.at[0, 0]
    rows = own.shape[0]
    fill_extended(ext_ref, own, upper_ref, lower_ref, incoming_ref)
    peers, slots = cross_ref.shape[:2]

    @pl.loop(0, peers)
    def _(peer):
        for turn in range(slots):
            row = rows + 2 * OVL + peer * slots + turn
            cross_ref[peer, turn] = row_product(blocks_ref, cols_ref, ext_ref, row).astype(BF)

    @pl.loop(0, OVL)
    def _(i):
        prev_ref[i] = row_product(blocks_ref, cols_ref, ext_ref, rows + i).astype(BF)
        next_ref[i] = row_product(blocks_ref, cols_ref, ext_ref, rows + OVL + i).astype(BF)


def own_kernel(cols_ref, own_ref, upper_ref, lower_ref, incoming_ref, blocks_ref, out_ref, ext_ref):
    own = own_ref.at[0, 0]
    rows = own.shape[0]
    fill_extended(ext_ref, own, upper_ref, lower_ref, incoming_ref)

    @pl.loop(0, rows // 2)
    def _(i):
        for j in range(2):
            out_ref[2 * i + j] = row_product(blocks_ref, cols_ref, ext_ref, 2 * i + j).astype(BF)


def add_returns(total_ref, list_ref, count_ref, partial_ref, from_prev_ref, from_next_ref, returned_ref):
    rows = partial_ref.shape[0]
    peers, slots = returned_ref.shape[:2]
    total_ref[...] = partial_ref[...].astype(F32)
    total_ref[:OVL] += from_prev_ref[...].astype(F32)
    total_ref[rows - OVL :] += from_next_ref[...].astype(F32)
    for slot in range(peers * slots):
        row, used = slot_target(list_ref, count_ref, slot, slots)
        value = jnp.where(used, returned_ref[slot // slots, slot % slots].astype(F32), 0.0)
        total_ref[row] += value


def first_kernel(list_ref, count_ref, partial_ref, from_prev_ref, from_next_ref, returned_ref, first_ref, out_ref, head_ref, tail_ref, total_ref):
    add_returns(total_ref, list_ref, count_ref, partial_ref, from_prev_ref, from_next_ref, returned_ref)
    first = first_ref.at[0, 0]
    rows = first.shape[0]
    first[...] = total_ref[...].astype(BF)
    pack_rows(first, list_ref, count_ref, out_ref, out_ref.shape[1])
    head_ref[...] = first[:OVL]
    tail_ref[...] = first[rows - OVL :]


def residual_kernel(cols_ref, list_ref, count_ref, rhs_ref, own_ref, upper_ref, lower_ref, incoming_ref, blocks_ref, res_ref, out_ref, head_ref, tail_ref, ext_ref):
    own = own_ref.at[0, 0]
    rows = own.shape[0]
    fill_extended(ext_ref, own, upper_ref, lower_ref, incoming_ref)
    res = res_ref.at[0, 0]

    @pl.loop(0, rows // 2)
    def _(i):
        for j in range(2):
            row = 2 * i + j
            image = row_product(blocks_ref, cols_ref, ext_ref, row)
            res[row] = (rhs_ref[0, 0, row].astype(F32) - image).astype(BF)

    pack_rows(res, list_ref, count_ref, out_ref, out_ref.shape[1])
    head_ref[...] = res[:OVL]
    tail_ref[...] = res[rows - OVL :]


def second_kernel(list_ref, count_ref, first_ref, partial_ref, from_prev_ref, from_next_ref, returned_ref, second_ref, total_ref):
    add_returns(total_ref, list_ref, count_ref, partial_ref, from_prev_ref, from_next_ref, returned_ref)
    second_ref[0, 0] = (first_ref[0, 0].astype(F32) + total_ref[...]).astype(BF)


def to_next(x):
    count = lax.axis_size("slab")
    return lax.ppermute(x, "slab", [(i, i + 1) for i in range(count - 1)])


def to_prev(x):
    count = lax.axis_size("slab")
    return lax.ppermute(x, "slab", [(i + 1, i) for i in range(count - 1)])


def route(buffer):
    return lax.all_to_all(buffer, "cross", split_axis=0, concat_axis=0, tiled=True)


def per_device(rhs, m_blocks, m_cols, j_blocks, j_cols, send_list, send_count):
    _, _, rows, block, vectors = rhs.shape
    peers, slots = send_list.shape[2:]
    extended_rows = m_blocks.shape[2]
    terms = m_blocks.shape[3]
    tile = block * vectors
    field_t = pltpu.VMEM(rhs.shape, BF)
    packed_t = pltpu.VMEM((peers, slots, block, vectors), BF)
    edge_t = pltpu.VMEM((OVL, block, vectors), BF)
    partial_t = pltpu.VMEM((rows, block, vectors), BF)
    ext_s = pltpu.VMEM((extended_rows, block, vectors), BF)
    total_s = pltpu.VMEM((rows, block, vectors), F32)

    rhs_v = in_vmem(rhs)
    m_v = in_vmem(m_blocks)
    j_v = in_vmem(j_blocks)

    packed, head, tail = pl.pallas_call(
        pack_rhs_kernel,
        out_shape=(packed_t, edge_t, edge_t),
        in_specs=[SM, SM, VM],
        out_specs=(VM, VM, VM),
        compiler_params=params(),
        cost_estimate=cost(0, 4 * rows * tile),
        name="pack_rhs",
    )(send_list, send_count, rhs_v)

    def extension(packed, head, tail):
        incoming = in_vmem(route(packed))
        upper = in_vmem(to_next(tail))
        lower = in_vmem(to_prev(head))
        return upper, lower, incoming

    def precondition(field, upper, lower, incoming):
        to_p, to_n, cross = pl.pallas_call(
            margin_kernel,
            out_shape=(edge_t, edge_t, packed_t),
            in_specs=[SM, VM, VM, VM, VM, VM],
            out_specs=(VM, VM, VM),
            scratch_shapes=[ext_s],
            compiler_params=params(),
            cost_estimate=cost(2 * (extended_rows - rows) * terms * block * tile, 6 * extended_rows * tile),
            name="margin_partial",
        )(m_cols, field, upper, lower, incoming, m_v)
        returned = in_vmem(route(cross))
        from_next = in_vmem(to_prev(to_p))
        from_prev = in_vmem(to_next(to_n))
        own = pl.pallas_call(
            own_kernel,
            out_shape=partial_t,
            in_specs=[SM, VM, VM, VM, VM, VM],
            out_specs=VM,
            scratch_shapes=[ext_s],
            compiler_params=params(),
            cost_estimate=cost(2 * rows * terms * block * tile, 6 * extended_rows * tile),
            name="own_partial",
        )(m_cols, field, upper, lower, incoming, m_v)
        return own, from_prev, from_next, returned

    upper, lower, incoming = extension(packed, head, tail)
    own, from_prev, from_next, returned = precondition(rhs_v, upper, lower, incoming)
    first, packed, head, tail = pl.pallas_call(
        first_kernel,
        out_shape=(field_t, packed_t, edge_t, edge_t),
        in_specs=[SM, SM, VM, VM, VM, VM],
        out_specs=(VM, VM, VM, VM),
        scratch_shapes=[total_s],
        compiler_params=params(),
        cost_estimate=cost(0, 10 * rows * tile),
        name="assemble_first",
    )(send_list, send_count, own, from_prev, from_next, returned)
    upper, lower, incoming = extension(packed, head, tail)
    residual, packed, head, tail = pl.pallas_call(
        residual_kernel,
        out_shape=(field_t, packed_t, edge_t, edge_t),
        in_specs=[SM, SM, SM, VM, VM, VM, VM, VM, VM],
        out_specs=(VM, VM, VM, VM),
        scratch_shapes=[ext_s],
        compiler_params=params(),
        cost_estimate=cost(2 * rows * terms * block * tile, 6 * extended_rows * tile),
        name="residual",
    )(j_cols, send_list, send_count, rhs_v, first, upper, lower, incoming, j_v)
    upper, lower, incoming = extension(packed, head, tail)
    own, from_prev, from_next, returned = precondition(residual, upper, lower, incoming)
    return pl.pallas_call(
        second_kernel,
        out_shape=jax.ShapeDtypeStruct(rhs.shape, BF),
        in_specs=[SM, SM, VM, VM, VM, VM, VM],
        out_specs=VM,
        scratch_shapes=[total_s],
        compiler_params=params(),
        cost_estimate=cost(0, 10 * rows * tile),
        name="assemble_second",
    )(send_list, send_count, first, own, from_prev, from_next, returned)


def solution(mesh):
    return jax.shard_map(
        per_device,
        mesh=mesh,
        in_specs=(
            P("slab", "cross", None, None, None),
            P("slab", "cross", None, None, None, None),
            P("slab", "cross", None, None),
            P("slab", "cross", None, None, None, None),
            P("slab", "cross", None, None),
            P("slab", "cross", None, None),
            P("slab", "cross", None),
        ),
        out_specs=P("slab", "cross", None, None, None),
        check_vma=False,
    )
```

```python
import functools

import jax
import jax.numpy as jnp
from jax import lax
from jax.experimental import pallas as pl
from jax.experimental.pallas import tpu as pltpu
from jax.sharding import PartitionSpec as P

OVL = 4
GROUP = 8
BF = jnp.bfloat16
F32 = jnp.float32
ANY = pl.BlockSpec(memory_space=pl.ANY)
DMA = pltpu.SemaphoreType.DMA


def params():
    return pltpu.CompilerParams(vmem_limit_bytes=63 * 1024 * 1024)


def cost(flops, nbytes):
    return pl.CostEstimate(flops=flops, bytes_accessed=nbytes, transcendentals=0)


def start(source, target, sem):
    copy = pltpu.make_async_copy(source, target, sem)
    copy.start()
    return copy


def wait_all(copies):
    for copy in copies:
        copy.wait()


def slot_target(list_ref, count_ref, slot):
    slots = list_ref.shape[2]
    peer, turn = slot // slots, slot % slots
    return list_ref[0, 0, turn, peer], turn < count_ref[0, 0, peer]


def start_packing(field, zero_ref, out_ref, list_ref, count_ref, sems):
    slots = out_ref.shape[1]
    copies = []
    for slot in range(out_ref.shape[0] * slots):
        row, used = slot_target(list_ref, count_ref, slot)
        target = out_ref.at[slot // slots, slot % slots]

        @pl.when(used)
        def _():
            pltpu.make_async_copy(field.at[row], target, sems.at[slot]).start()

        @pl.when(jnp.logical_not(used))
        def _():
            pltpu.make_async_copy(zero_ref, target, sems.at[slot]).start()

        copies.append(pltpu.make_async_copy(zero_ref, target, sems.at[slot]))
    return copies


def start_lists(list_hbm, count_hbm, list_ref, count_ref, sems):
    return [start(list_hbm, list_ref, sems.at[0]), start(count_hbm, count_ref, sems.at[1])]


def pack_rhs_kernel(list_hbm, count_hbm, rhs_hbm, out_hbm, head_hbm, tail_hbm, list_ref, count_ref, zero_ref, field_ref, in_sem, out_sem, row_sem):
    lists = start_lists(list_hbm, count_hbm, list_ref, count_ref, in_sem)
    field = start(rhs_hbm.at[0, 0], field_ref, in_sem.at[2])
    rows = field_ref.shape[0]
    zero_ref[...] = jnp.zeros_like(zero_ref)
    wait_all(lists)
    field.wait()
    copies = start_packing(field_ref, zero_ref, out_hbm, list_ref, count_ref, row_sem)
    copies.append(start(field_ref.at[pl.ds(0, OVL)], head_hbm, out_sem.at[0]))
    copies.append(start(field_ref.at[pl.ds(rows - OVL, OVL)], tail_hbm, out_sem.at[1]))
    wait_all(copies)


def start_extended(own, upper, lower, incoming, ext_ref, sems):
    rows = own.shape[0]
    copies = [
        start(own, ext_ref.at[pl.ds(0, rows)], sems.at[0]),
        start(incoming, ext_ref.at[pl.ds(rows + 2 * OVL, incoming.shape[0])], sems.at[3]),
        start(upper, ext_ref.at[pl.ds(rows, OVL)], sems.at[1]),
        start(lower, ext_ref.at[pl.ds(rows + OVL, OVL)], sems.at[2]),
    ]
    return copies


def start_blocks(blocks_hbm, first, chunk_ref, sems):
    copies = []
    for g in range(chunk_ref.shape[0] // GROUP):
        source = blocks_hbm.at[0, 0, pl.ds(first + g * GROUP, GROUP)]
        copies.append(start(source, chunk_ref.at[pl.ds(g * GROUP, GROUP)], sems.at[g]))
    return copies


def row_product(chunk_ref, index, cols_ref, row, ext_ref):
    terms = chunk_ref.shape[1]
    left = jnp.concatenate([chunk_ref[index, k] for k in range(terms)], axis=1)
    right = jnp.concatenate([ext_ref[cols_ref[0, k, 0, row]] for k in range(terms)], axis=0)
    return jnp.dot(left, right, preferred_element_type=F32)


def margin_kernel(cols_hbm, own_hbm, upper_hbm, lower_hbm, incoming_hbm, blocks_hbm, prev_hbm, next_hbm, cross_hbm, cols_ref, ext_ref, chunk_ref, part_ref, in_sem, block_sem, out_sem):
    own = own_hbm.at[0, 0]
    rows = own.shape[0]
    cols = start(cols_hbm, cols_ref, in_sem.at[4])
    pieces = start_extended(own, upper_hbm, lower_hbm, incoming_hbm, ext_ref, in_sem)
    blocks = start_blocks(blocks_hbm, rows, chunk_ref, block_sem)
    cols.wait()
    wait_all(pieces)
    copies = []
    for g, block in enumerate(blocks):
        block.wait()
        for j in range(GROUP):
            i = g * GROUP + j
            part_ref[i] = row_product(chunk_ref, i, cols_ref, rows + i, ext_ref).astype(BF)
        if g == 0:
            copies.append(start(part_ref.at[pl.ds(0, OVL)], prev_hbm, out_sem.at[0]))
            copies.append(start(part_ref.at[pl.ds(OVL, OVL)], next_hbm, out_sem.at[1]))
        else:
            source = part_ref.at[pl.ds(g * GROUP, GROUP)]
            target = cross_hbm.at[pl.ds(g * GROUP - 2 * OVL, GROUP)]
            copies.append(start(source, target, out_sem.at[g + 1]))
    wait_all(copies)


def own_kernel(cols_hbm, own_hbm, upper_hbm, lower_hbm, incoming_hbm, blocks_hbm, out_hbm, cols_ref, ext_ref, chunk_ref, part_ref, in_sem, block_sem, out_sem):
    own = own_hbm.at[0, 0]
    cols = start(cols_hbm, cols_ref, in_sem.at[4])
    pieces = start_extended(own, upper_hbm, lower_hbm, incoming_hbm, ext_ref, in_sem)
    blocks = start_blocks(blocks_hbm, 0, chunk_ref, block_sem)
    cols.wait()
    wait_all(pieces)
    copies = []
    for g, block in enumerate(blocks):
        block.wait()
        for j in range(GROUP):
            i = g * GROUP + j
            part_ref[i] = row_product(chunk_ref, i, cols_ref, i, ext_ref).astype(BF)
        rows = pl.ds(g * GROUP, GROUP)
        copies.append(start(part_ref.at[rows], out_hbm.at[rows], out_sem.at[g]))
    wait_all(copies)


def start_returns(partial_hbm, from_prev_hbm, from_next_hbm, returned_hbm, partial_ref, edge_ref, returned_ref, sems):
    return [
        start(partial_hbm, partial_ref, sems.at[2]),
        start(from_prev_hbm, edge_ref.at[0], sems.at[3]),
        start(from_next_hbm, edge_ref.at[1], sems.at[4]),
        start(returned_hbm, returned_ref, sems.at[5]),
    ]


def add_returns(total_ref, list_ref, count_ref, copies, partial_ref, edge_ref, returned_ref):
    rows = partial_ref.shape[0]
    copies[0].wait()
    total_ref[...] = partial_ref[...].astype(F32)
    copies[1].wait()
    total_ref[:OVL] += edge_ref[0].astype(F32)
    copies[2].wait()
    total_ref[rows - OVL :] += edge_ref[1].astype(F32)
    copies[3].wait()
    for slot in range(returned_ref.shape[0]):
        row, used = slot_target(list_ref, count_ref, slot)

        @pl.when(used)
        def _():
            total_ref[row] += returned_ref[slot].astype(F32)


def first_kernel(list_hbm, count_hbm, partial_hbm, from_prev_hbm, from_next_hbm, returned_hbm, first_hbm, out_hbm, head_hbm, tail_hbm, list_ref, count_ref, zero_ref, partial_ref, edge_ref, returned_ref, total_ref, in_sem, out_sem, row_sem):
    lists = start_lists(list_hbm, count_hbm, list_ref, count_ref, in_sem)
    copies = start_returns(partial_hbm, from_prev_hbm, from_next_hbm, returned_hbm, partial_ref, edge_ref, returned_ref, in_sem)
    zero_ref[...] = jnp.zeros_like(zero_ref)
    wait_all(lists)
    add_returns(total_ref, list_ref, count_ref, copies, partial_ref, edge_ref, returned_ref)
    partial_ref[...] = total_ref[...].astype(BF)
    finish_field(partial_ref, zero_ref, first_hbm, out_hbm, head_hbm, tail_hbm, list_ref, count_ref, out_sem, row_sem)


def finish_field(field_ref, zero_ref, field_hbm, out_hbm, head_hbm, tail_hbm, list_ref, count_ref, out_sem, row_sem):
    rows = field_ref.shape[0]
    copies = start_packing(field_ref, zero_ref, out_hbm, list_ref, count_ref, row_sem)
    copies.append(start(field_ref.at[pl.ds(0, OVL)], head_hbm, out_sem.at[0]))
    copies.append(start(field_ref.at[pl.ds(rows - OVL, OVL)], tail_hbm, out_sem.at[1]))
    copies.append(start(field_ref, field_hbm.at[0, 0], out_sem.at[2]))
    wait_all(copies)


def residual_kernel(cols_hbm, list_hbm, count_hbm, rhs_hbm, own_hbm, upper_hbm, lower_hbm, incoming_hbm, blocks_hbm, res_hbm, out_hbm, head_hbm, tail_hbm, cols_ref, list_ref, count_ref, zero_ref, rhs_ref, ext_ref, chunk_ref, in_sem, ext_sem, block_sem, out_sem, row_sem):
    own = own_hbm.at[0, 0]
    cols = start(cols_hbm, cols_ref, ext_sem.at[4])
    lists = start_lists(list_hbm, count_hbm, list_ref, count_ref, in_sem)
    pieces = start_extended(own, upper_hbm, lower_hbm, incoming_hbm, ext_ref, ext_sem)
    pieces.append(start(rhs_hbm.at[0, 0], rhs_ref, in_sem.at[2]))
    blocks = start_blocks(blocks_hbm, 0, chunk_ref, block_sem)
    zero_ref[...] = jnp.zeros_like(zero_ref)
    cols.wait()
    wait_all(lists)
    wait_all(pieces)
    for g, block in enumerate(blocks):
        block.wait()
        for j in range(GROUP):
            i = g * GROUP + j
            image = row_product(chunk_ref, i, cols_ref, i, ext_ref)
            rhs_ref[i] = (rhs_ref[i].astype(F32) - image).astype(BF)
    finish_field(rhs_ref, zero_ref, res_hbm, out_hbm, head_hbm, tail_hbm, list_ref, count_ref, out_sem, row_sem)


def second_kernel(list_hbm, count_hbm, first_hbm, partial_hbm, from_prev_hbm, from_next_hbm, returned_hbm, second_hbm, list_ref, count_ref, first_ref, partial_ref, edge_ref, returned_ref, total_ref, in_sem, out_sem):
    lists = start_lists(list_hbm, count_hbm, list_ref, count_ref, in_sem)
    copies = start_returns(partial_hbm, from_prev_hbm, from_next_hbm, returned_hbm, partial_ref, edge_ref, returned_ref, in_sem)
    base = start(first_hbm.at[0, 0], first_ref, in_sem.at[6])
    wait_all(lists)
    add_returns(total_ref, list_ref, count_ref, copies, partial_ref, edge_ref, returned_ref)
    base.wait()
    stores = []
    rows = first_ref.shape[0]
    for g in range(rows // GROUP):
        part = pl.ds(g * GROUP, GROUP)
        first_ref[part] = (first_ref[part].astype(F32) + total_ref[part]).astype(BF)
        stores.append(start(first_ref.at[part], second_hbm.at[0, 0, part], out_sem.at[g]))
    wait_all(stores)


def to_next(x):
    count = lax.axis_size("slab")
    return lax.ppermute(x, "slab", [(i, i + 1) for i in range(count - 1)])


def to_prev(x):
    count = lax.axis_size("slab")
    return lax.ppermute(x, "slab", [(i + 1, i) for i in range(count - 1)])


def route(buffer):
    return lax.all_to_all(buffer, "cross", split_axis=0, concat_axis=0, tiled=True)


def per_device(rhs, m_blocks, m_cols, j_blocks, j_cols, send_list, send_count):
    _, _, rows, block, vectors = rhs.shape
    peers, slots = send_list.shape[2:]
    listed = peers * slots
    extended_rows, terms = m_blocks.shape[2:4]
    margin_rows = extended_rows - rows
    tile = block * vectors
    out = jax.ShapeDtypeStruct
    field_t = out(rhs.shape, BF)
    packed_t = out((peers, slots, block, vectors), BF)
    edge_t = out((OVL, block, vectors), BF)
    partial_t = out((rows, block, vectors), BF)
    listed_t = out((listed, block, vectors), BF)

    m_cols = jnp.transpose(m_cols, (0, 3, 1, 2))
    j_cols = jnp.transpose(j_cols, (0, 3, 1, 2))
    send_list = jnp.transpose(send_list, (0, 1, 3, 2))

    def smem(x):
        return pltpu.SMEM(x.shape, jnp.int32)

    def tiles(count, dtype=BF):
        return pltpu.VMEM((count, block, vectors), dtype)

    def chunk(count):
        return pltpu.VMEM((count, terms, block, block), BF)

    lists = [smem(send_list), smem(send_count)]
    zero = pltpu.VMEM((block, vectors), BF)
    edges = pltpu.VMEM((2, OVL, block, vectors), BF)

    def call(kernel, name, out_shape, scratch, estimate, *operands):
        return pl.pallas_call(
            kernel,
            out_shape=out_shape,
            in_specs=[ANY] * len(operands),
            out_specs=jax.tree.map(lambda _: ANY, out_shape),
            scratch_shapes=scratch,
            compiler_params=params(),
            cost_estimate=estimate,
            name=name,
        )(*operands)

    packed, head, tail = call(
        pack_rhs_kernel,
        "pack_rhs",
        (packed_t, edge_t, edge_t),
        [*lists, zero, tiles(rows), DMA((3,)), DMA((2,)), DMA((listed,))],
        cost(0, 4 * rows * tile),
        send_list,
        send_count,
        rhs,
    )

    def extension(packed, head, tail):
        incoming = route(packed).reshape(listed, block, vectors)
        return to_next(tail), to_prev(head), incoming

    def precondition(field, upper, lower, incoming):
        to_p, to_n, cross = call(
            margin_kernel,
            "margin_partial",
            (edge_t, edge_t, listed_t),
            [smem(m_cols), tiles(extended_rows), chunk(margin_rows), tiles(margin_rows), DMA((5,)), DMA((margin_rows // GROUP,)), DMA((margin_rows // GROUP + 1,))],
            cost(2 * margin_rows * terms * block * tile, 12 * extended_rows * tile),
            m_cols,
            field,
            upper,
            lower,
            incoming,
            m_blocks,
        )
        returned = route(cross.reshape(peers, slots, block, vectors)).reshape(listed, block, vectors)
        from_next = to_prev(to_p)
        from_prev = to_next(to_n)
        own = call(
            own_kernel,
            "own_partial",
            partial_t,
            [smem(m_cols), tiles(extended_rows), chunk(rows), tiles(rows), DMA((5,)), DMA((rows // GROUP,)), DMA((rows // GROUP,))],
            cost(2 * rows * terms * block * tile, 12 * extended_rows * tile),
            m_cols,
            field,
            upper,
            lower,
            incoming,
            m_blocks,
        )
        return own, from_prev, from_next, returned

    upper, lower, incoming = extension(packed, head, tail)
    own, from_prev, from_next, returned = precondition(rhs, upper, lower, incoming)
    first, packed, head, tail = call(
        first_kernel,
        "assemble_first",
        (field_t, packed_t, edge_t, edge_t),
        [*lists, zero, tiles(rows), edges, tiles(listed), tiles(rows, F32), DMA((6,)), DMA((3,)), DMA((listed,))],
        cost(0, 10 * rows * tile),
        send_list,
        send_count,
        own,
        from_prev,
        from_next,
        returned,
    )
    upper, lower, incoming = extension(packed, head, tail)
    residual, packed, head, tail = call(
        residual_kernel,
        "residual",
        (field_t, packed_t, edge_t, edge_t),
        [smem(j_cols), *lists, zero, tiles(rows), tiles(extended_rows), chunk(rows), DMA((3,)), DMA((5,)), DMA((rows // GROUP,)), DMA((3,)), DMA((listed,))],
        cost(2 * rows * terms * block * tile, 12 * extended_rows * tile),
        j_cols,
        send_list,
        send_count,
        rhs,
        first,
        upper,
        lower,
        incoming,
        j_blocks,
    )
    upper, lower, incoming = extension(packed, head, tail)
    own, from_prev, from_next, returned = precondition(residual, upper, lower, incoming)
    return call(
        second_kernel,
        "assemble_second",
        field_t,
        [*lists, tiles(rows), tiles(rows), edges, tiles(listed), tiles(rows, F32), DMA((7,)), DMA((rows // GROUP,))],
        cost(0, 10 * rows * tile),
        send_list,
        send_count,
        first,
        own,
        from_prev,
        from_next,
        returned,
    )


def solution(mesh):
    return jax.shard_map(
        per_device,
        mesh=mesh,
        in_specs=(
            P("slab", "cross", None, None, None),
            P("slab", "cross", None, None, None, None),
            P("slab", "cross", None, None),
            P("slab", "cross", None, None, None, None),
            P("slab", "cross", None, None),
            P("slab", "cross", None, None),
            P("slab", "cross", None),
        ),
        out_specs=P("slab", "cross", None, None, None),
        check_vma=False,
    )
```

```python
import functools

import jax
import jax.numpy as jnp
from jax import lax
from jax.experimental import pallas as pl
from jax.experimental.pallas import tpu as pltpu
from jax.sharding import PartitionSpec as P

OVL = 4
GROUP = 8
BF = jnp.bfloat16
F32 = jnp.float32
HBM = pl.BlockSpec(memory_space=pltpu.HBM)
VMEM = pl.BlockSpec(memory_space=pltpu.VMEM)
DMA = pltpu.SemaphoreType.DMA


def params():
    return pltpu.CompilerParams(vmem_limit_bytes=36 * 1024 * 1024)


def cost(flops, nbytes):
    return pl.CostEstimate(flops=flops, bytes_accessed=nbytes, transcendentals=0)


def start(source, target, sem):
    copy = pltpu.make_async_copy(source, target, sem)
    copy.start()
    return copy


def wait_all(copies):
    for copy in copies:
        copy.wait()


def slot_target(list_ref, count_ref, slot):
    slots = list_ref.shape[2]
    peer, turn = slot // slots, slot % slots
    return list_ref[0, 0, turn, peer], turn < count_ref[0, 0, peer]


def start_packing(field_ref, packed_ref, out_hbm, list_ref, count_ref, sems):
    slots = out_hbm.shape[1]
    peers = GROUP // slots
    copies = []
    for g in range(packed_ref.shape[0] // GROUP):
        for slot in range(g * GROUP, (g + 1) * GROUP):
            row, used = slot_target(list_ref, count_ref, slot)
            packed_ref[slot] = jnp.where(used, field_ref[row], jnp.zeros((), BF))
        for peer in range(g * peers, (g + 1) * peers):
            copies.append(start(packed_ref.at[pl.ds(peer * slots, slots)], out_hbm.at[peer], sems.at[peer]))
    return copies


def start_lists(list_hbm, count_hbm, list_ref, count_ref, sems):
    return [start(list_hbm, list_ref, sems.at[0]), start(count_hbm, count_ref, sems.at[1])]


def pack_rhs_kernel(list_hbm, count_hbm, rhs_hbm, out_hbm, head_hbm, tail_hbm, list_ref, count_ref, packed_ref, field_ref, in_sem, out_sem, row_sem):
    lists = start_lists(list_hbm, count_hbm, list_ref, count_ref, in_sem)
    field = start(rhs_hbm.at[0, 0], field_ref, in_sem.at[2])
    rows = field_ref.shape[0]
    wait_all(lists)
    field.wait()
    copies = start_packing(field_ref, packed_ref, out_hbm, list_ref, count_ref, row_sem)
    copies.append(start(field_ref.at[pl.ds(0, OVL)], head_hbm, out_sem.at[0]))
    copies.append(start(field_ref.at[pl.ds(rows - OVL, OVL)], tail_hbm, out_sem.at[1]))
    wait_all(copies)


def start_blocks(blocks_hbm, first, chunk_ref, sems, order):
    copies = []
    for g in order:
        source = blocks_hbm.at[0, 0, pl.ds(first + g * GROUP, GROUP)]
        copies.append(start(source, chunk_ref.at[pl.ds(g * GROUP, GROUP)], sems.at[g]))
    return copies


def picked_product(chunk_ref, index, terms, picks, ext_ref):
    left = jnp.concatenate([chunk_ref[index, k] for k in terms], axis=1)
    right = jnp.concatenate([ext_ref[pick] for pick in picks], axis=0)
    return jnp.dot(left, right, preferred_element_type=F32)


def row_product(chunk_ref, index, cols_ref, row, ext_ref):
    terms = range(chunk_ref.shape[1])
    return picked_product(chunk_ref, index, terms, [cols_ref[0, k, 0, row] for k in terms], ext_ref)


def stage_kernel(own_hbm, upper_hbm, lower_hbm, near_ref, sems):
    rows = own_hbm.shape[2]
    wait_all([
        start(own_hbm.at[0, 0], near_ref.at[pl.ds(0, rows)], sems.at[0]),
        start(upper_hbm, near_ref.at[pl.ds(rows, OVL)], sems.at[1]),
        start(lower_hbm, near_ref.at[pl.ds(rows + OVL, OVL)], sems.at[2]),
    ])


def half_row(low_ref, high_ref, row):
    half = low_ref.shape[0]
    return low_ref.at[row] if row < half else high_ref.at[row - half]


def near_residual_kernel(cols_hbm, blocks_hbm, rhs_hbm, own_hbm, upper_hbm, lower_hbm, low_ref, high_ref, cols_ref, ext_ref, chunk_ref, rhs_ref, in_sem, cols_sem, block_sem):
    rows = rhs_ref.shape[0]
    near = ext_ref.shape[0] - 1
    cols = start(cols_hbm, cols_ref, cols_sem.at[0])
    pieces = start_near(own_hbm, upper_hbm, lower_hbm, ext_ref, in_sem)
    pieces.append(start(rhs_hbm.at[0, 0], rhs_ref, in_sem.at[3]))
    groups = range(rows // GROUP)
    blocks = start_blocks(blocks_hbm, 0, chunk_ref, block_sem, groups)
    ext_ref[near] = jnp.zeros_like(ext_ref[near])
    cols.wait()
    wait_all(pieces)
    terms = chunk_ref.shape[1]
    for g, block in zip(groups, blocks):
        block.wait()
        for j in range(GROUP):
            i = g * GROUP + j
            picks = [jnp.minimum(cols_ref[0, k, 0, i], near) for k in range(terms)]
            half_row(low_ref, high_ref, i)[...] = rhs_ref[i].astype(F32) - picked_product(chunk_ref, i, range(terms), picks, ext_ref)


def fill_extended(near_ref, incoming_ref, ext_ref):
    near = near_ref.shape[0]
    ext_ref[:near] = near_ref[...]
    ext_ref[near:] = incoming_ref[...]


def margin_kernel(cols_hbm, blocks_hbm, near_ref, incoming_ref, cross_hbm, cols_ref, ext_ref, chunk_ref, part_ref, in_sem, block_sem, out_sem):
    cols = start(cols_hbm, cols_ref, in_sem.at[0])
    near = near_ref.shape[0]
    groups = range(chunk_ref.shape[0] // GROUP)
    blocks = start_blocks(blocks_hbm, near, chunk_ref, block_sem, groups)
    fill_extended(near_ref, incoming_ref, ext_ref)
    cols.wait()
    copies = []
    for g, block in zip(groups, blocks):
        block.wait()
        for j in range(GROUP):
            i = g * GROUP + j
            part_ref[i] = row_product(chunk_ref, i, cols_ref, near + i, ext_ref).astype(BF)
        part = pl.ds(g * GROUP, GROUP)
        copies.append(start(part_ref.at[part], cross_hbm.at[part], out_sem.at[g]))
    wait_all(copies)


def start_near(own_hbm, upper_hbm, lower_hbm, ext_ref, sems):
    rows = own_hbm.shape[2]
    return [
        start(own_hbm.at[0, 0], ext_ref.at[pl.ds(0, rows)], sems.at[0]),
        start(upper_hbm, ext_ref.at[pl.ds(rows, OVL)], sems.at[1]),
        start(lower_hbm, ext_ref.at[pl.ds(rows + OVL, OVL)], sems.at[2]),
    ]


def own_kernel(cols_hbm, blocks_hbm, own_hbm, upper_hbm, lower_hbm, incoming_ref, part_ref, prev_hbm, next_hbm, cols_ref, ext_ref, chunk_ref, edge_ref, in_sem, cols_sem, block_sem, out_sem):
    rows = part_ref.shape[0]
    cols = start(cols_hbm, cols_ref, cols_sem.at[0])
    pieces = start_near(own_hbm, upper_hbm, lower_hbm, ext_ref, in_sem)
    last = rows // GROUP
    order = [last, *range(last)]
    blocks = start_blocks(blocks_hbm, 0, chunk_ref, block_sem, order)
    ext_ref[rows + 2 * OVL :] = incoming_ref[...]
    cols.wait()
    wait_all(pieces)
    copies = []
    for g, block in zip(order, blocks):
        block.wait()
        for j in range(GROUP):
            i = g * GROUP + j
            value = row_product(chunk_ref, i, cols_ref, i, ext_ref).astype(BF)
            if g == last:
                edge_ref[j] = value
            else:
                part_ref[i] = value
        if g == last:
            copies.append(start(edge_ref.at[pl.ds(0, OVL)], prev_hbm, out_sem.at[0]))
            copies.append(start(edge_ref.at[pl.ds(OVL, OVL)], next_hbm, out_sem.at[1]))
    wait_all(copies)


def add_returns(sum_ref, list_ref, count_ref, lists, edges, edge_ref, part_ref, returned_ref):
    rows = part_ref.shape[0]
    sum_ref[...] = part_ref[...].astype(F32)
    wait_all(lists)
    for slot in range(returned_ref.shape[0]):
        row, used = slot_target(list_ref, count_ref, slot)
        sum_ref[row] += jnp.where(used, returned_ref[slot].astype(F32), 0.0)

    wait_all(edges)
    sum_ref[:OVL] += edge_ref[0].astype(F32)
    sum_ref[rows - OVL :] += edge_ref[1].astype(F32)


def start_edges(from_prev_hbm, from_next_hbm, edge_ref, sems):
    return [start(from_prev_hbm, edge_ref.at[0], sems.at[0]), start(from_next_hbm, edge_ref.at[1], sems.at[1])]


def first_kernel(list_hbm, count_hbm, from_prev_hbm, from_next_hbm, part_ref, returned_ref, first_hbm, out_hbm, head_hbm, tail_hbm, list_ref, count_ref, edge_ref, packed_ref, field_ref, sum_ref, in_sem, edge_sem, out_sem, row_sem):
    lists = start_lists(list_hbm, count_hbm, list_ref, count_ref, in_sem)
    edges = start_edges(from_prev_hbm, from_next_hbm, edge_ref, edge_sem)
    add_returns(sum_ref, list_ref, count_ref, lists, edges, edge_ref, part_ref, returned_ref)
    field_ref[...] = sum_ref[...].astype(BF)
    finish_field(field_ref, packed_ref, first_hbm, out_hbm, head_hbm, tail_hbm, list_ref, count_ref, out_sem, row_sem)


def finish_field(field_ref, packed_ref, field_hbm, out_hbm, head_hbm, tail_hbm, list_ref, count_ref, out_sem, row_sem):
    rows = field_ref.shape[0]
    copies = [start(field_ref, field_hbm.at[0, 0], out_sem.at[2])]
    copies += start_packing(field_ref, packed_ref, out_hbm, list_ref, count_ref, row_sem)
    copies.append(start(field_ref.at[pl.ds(0, OVL)], head_hbm, out_sem.at[0]))
    copies.append(start(field_ref.at[pl.ds(rows - OVL, OVL)], tail_hbm, out_sem.at[1]))
    wait_all(copies)


def listed_residual_kernel(near, cols_hbm, list_hbm, count_hbm, blocks_hbm, low_ref, high_ref, incoming_ref, out_hbm, cols_ref, list_ref, count_ref, packed_ref, ext_ref, chunk_ref, res_ref, in_sem, cols_sem, block_sem, row_sem):
    cols = start(cols_hbm, cols_ref, cols_sem.at[0])
    groups = range(res_ref.shape[0] // GROUP)
    terms = chunk_ref.shape[1]
    blocks = []
    for g in groups:
        part = pl.ds(g * GROUP, GROUP)
        blocks.append(start(blocks_hbm.at[0, 0, part, pl.ds(1, terms)], chunk_ref.at[part], block_sem.at[g]))
    lists = start_lists(list_hbm, count_hbm, list_ref, count_ref, in_sem)
    listed = incoming_ref.shape[0]
    ext_ref[:listed] = incoming_ref[...]
    ext_ref[listed] = jnp.zeros_like(ext_ref[listed])
    cols.wait()
    for g, block in zip(groups, blocks):
        block.wait()
        for j in range(GROUP):
            i = g * GROUP + j
            named = [cols_ref[0, k + 1, 0, i] for k in range(terms)]
            picks = [jnp.where(col >= near, col - near, listed) for col in named]
            image = picked_product(chunk_ref, i, range(terms), picks, ext_ref)
            res_ref[i] = (half_row(low_ref, high_ref, i)[...] - image).astype(BF)
    wait_all(lists)
    wait_all(start_packing(res_ref, packed_ref, out_hbm, list_ref, count_ref, row_sem))


def own_residual_kernel(cols_hbm, blocks_hbm, rhs_hbm, own_hbm, upper_hbm, lower_hbm, incoming_ref, res_hbm, head_hbm, tail_hbm, cols_ref, ext_ref, chunk_ref, res_ref, in_sem, cols_sem, block_sem, out_sem):
    rows = res_ref.shape[0]
    cols = start(cols_hbm, cols_ref, cols_sem.at[0])
    pieces = start_near(own_hbm, upper_hbm, lower_hbm, ext_ref, in_sem)
    pieces.append(start(rhs_hbm.at[0, 0], res_ref, in_sem.at[3]))
    groups = range(rows // GROUP)
    blocks = start_blocks(blocks_hbm, 0, chunk_ref, block_sem, groups)
    ext_ref[rows + 2 * OVL :] = incoming_ref[...]
    cols.wait()
    wait_all(pieces)
    for g, block in zip(groups, blocks):
        block.wait()
        for j in range(GROUP):
            i = g * GROUP + j
            image = row_product(chunk_ref, i, cols_ref, i, ext_ref)
            res_ref[i] = (res_ref[i].astype(F32) - image).astype(BF)
    wait_all([
        start(res_ref.at[pl.ds(0, OVL)], head_hbm, out_sem.at[0]),
        start(res_ref.at[pl.ds(rows - OVL, OVL)], tail_hbm, out_sem.at[1]),
        start(res_ref, res_hbm.at[0, 0], out_sem.at[2]),
    ])


def second_kernel(list_hbm, count_hbm, from_prev_hbm, from_next_hbm, first_hbm, part_ref, returned_ref, second_hbm, list_ref, count_ref, edge_ref, field_ref, sum_ref, in_sem, edge_sem, out_sem):
    lists = start_lists(list_hbm, count_hbm, list_ref, count_ref, in_sem)
    edges = start_edges(from_prev_hbm, from_next_hbm, edge_ref, edge_sem)
    base = start(first_hbm.at[0, 0], field_ref, in_sem.at[2])
    add_returns(sum_ref, list_ref, count_ref, lists, edges, edge_ref, part_ref, returned_ref)
    base.wait()
    stores = []
    for g in range(field_ref.shape[0] // GROUP):
        part = pl.ds(g * GROUP, GROUP)
        field_ref[part] = (field_ref[part].astype(F32) + sum_ref[part]).astype(BF)
        stores.append(start(field_ref.at[part], second_hbm.at[0, 0, part], out_sem.at[g]))
    wait_all(stores)


def to_next(x):
    count = lax.axis_size("slab")
    return lax.ppermute(x, "slab", [(i, i + 1) for i in range(count - 1)])


def to_prev(x):
    count = lax.axis_size("slab")
    return lax.ppermute(x, "slab", [(i + 1, i) for i in range(count - 1)])


def route(buffer):
    return lax.all_to_all(buffer, "cross", split_axis=0, concat_axis=0, tiled=True)


def per_device(rhs, m_blocks, m_cols, j_blocks, j_cols, send_list, send_count):
    _, _, rows, block, vectors = rhs.shape
    peers, slots = send_list.shape[2:]
    listed = peers * slots
    extended_rows, terms = m_blocks.shape[2:4]
    near_rows = rows + 2 * OVL
    groups = rows // GROUP
    tile = block * vectors
    field_t = pltpu.HBM(rhs.shape, BF)
    packed_t = pltpu.HBM((peers, slots, block, vectors), BF)
    edge_t = pltpu.HBM((OVL, block, vectors), BF)
    listed_t = pltpu.HBM((listed, block, vectors), BF)

    m_cols = jnp.transpose(m_cols, (0, 3, 1, 2))
    j_cols = jnp.transpose(j_cols, (0, 3, 1, 2))
    send_list = jnp.transpose(send_list, (0, 1, 3, 2))

    def smem(x):
        return pltpu.SMEM(x.shape, jnp.int32)

    def tiles(count, dtype=BF):
        return pltpu.VMEM((count, block, vectors), dtype)

    def chunk(count):
        return pltpu.VMEM((count, terms, block, block), BF)

    lists = [smem(send_list), smem(send_count)]
    edges = pltpu.VMEM((2, OVL, block, vectors), BF)

    def call(kernel, name, out_shape, scratch, estimate, *operands, staged=()):
        placed = [pltpu.with_memory_space_constraint(x, pltpu.HBM) for x in operands]
        placed += [pltpu.with_memory_space_constraint(x, pltpu.VMEM) for x in staged]
        spec = lambda t: pl.BlockSpec(memory_space=t.memory_space)
        return pl.pallas_call(
            kernel,
            out_shape=out_shape,
            in_specs=[HBM] * len(operands) + [VMEM] * len(staged),
            out_specs=tuple(map(spec, out_shape)) if isinstance(out_shape, tuple) else spec(out_shape),
            scratch_shapes=scratch,
            compiler_params=params(),
            cost_estimate=estimate,
            name=name,
        )(*placed)

    packed, head, tail = call(
        pack_rhs_kernel,
        "pack_rhs",
        (packed_t, edge_t, edge_t),
        [*lists, tiles(listed), tiles(rows), DMA((3,)), DMA((2,)), DMA((peers,))],
        cost(0, 4 * rows * tile),
        send_list,
        send_count,
        rhs,
    )

    def extension(packed, head, tail):
        incoming = route(packed).reshape(listed, block, vectors)
        return to_next(tail), to_prev(head), incoming

    def precondition(field, upper, lower, incoming):
        near = call(
            stage_kernel,
            "stage_margin",
            tiles(near_rows),
            [DMA((3,))],
            cost(0, 4 * near_rows * tile),
            field,
            upper,
            lower,
        )
        groups = listed // GROUP
        cross = call(
            margin_kernel,
            "slot_partial",
            listed_t,
            [smem(m_cols), tiles(extended_rows), chunk(listed), tiles(listed), DMA((1,)), DMA((groups,)), DMA((groups,))],
            cost(2 * listed * terms * block * tile, 12 * extended_rows * tile),
            m_cols,
            m_blocks,
            staged=(near, incoming),
        )
        returned = route(cross.reshape(peers, slots, block, vectors)).reshape(listed, block, vectors)
        groups = near_rows // GROUP
        part, to_p, to_n = call(
            own_kernel,
            "own_partial",
            (tiles(rows), edge_t, edge_t),
            [smem(m_cols), tiles(extended_rows), chunk(near_rows), tiles(2 * OVL), DMA((3,)), DMA((1,)), DMA((groups,)), DMA((2,))],
            cost(2 * near_rows * terms * block * tile, 12 * extended_rows * tile),
            m_cols,
            m_blocks,
            field,
            upper,
            lower,
            staged=(incoming,),
        )
        from_next = to_prev(to_p)
        from_prev = to_next(to_n)
        return part, from_prev, from_next, returned

    upper, lower, incoming = extension(packed, head, tail)
    part, from_prev, from_next, returned = precondition(rhs, upper, lower, incoming)
    first, packed, head, tail = call(
        first_kernel,
        "assemble_first",
        (field_t, packed_t, edge_t, edge_t),
        [*lists, edges, tiles(listed), tiles(rows), tiles(rows, F32), DMA((2,)), DMA((2,)), DMA((3,)), DMA((peers,))],
        cost(0, 10 * rows * tile),
        send_list,
        send_count,
        from_prev,
        from_next,
        staged=(part, returned),
    )
    upper, lower, incoming = extension(packed, head, tail)
    low, high = call(
        near_residual_kernel,
        "near_residual",
        (tiles(rows // 2, F32), tiles(rows // 2, F32)),
        [smem(j_cols), tiles(near_rows + 1), chunk(rows), tiles(rows), DMA((4,)), DMA((1,)), DMA((groups,))],
        cost(2 * rows * terms * block * tile, 4 * (near_rows + terms * rows) * tile),
        j_cols,
        j_blocks,
        rhs,
        first,
        upper,
        lower,
    )
    packed = call(
        functools.partial(listed_residual_kernel, near_rows),
        "listed_residual",
        packed_t,
        [smem(j_cols), *lists, tiles(listed), tiles(listed + 1), pltpu.VMEM((rows, terms - 1, block, block), BF), tiles(rows), DMA((2,)), DMA((1,)), DMA((groups,)), DMA((peers,))],
        cost(2 * rows * terms * block * tile, 12 * extended_rows * tile),
        j_cols,
        send_list,
        send_count,
        j_blocks,
        staged=(low, high, incoming),
    )
    residual, head, tail = call(
        own_residual_kernel,
        "own_residual",
        (field_t, edge_t, edge_t),
        [smem(j_cols), tiles(extended_rows), chunk(rows), tiles(rows), DMA((4,)), DMA((1,)), DMA((groups,)), DMA((3,))],
        cost(2 * rows * terms * block * tile, 12 * extended_rows * tile),
        j_cols,
        j_blocks,
        rhs,
        first,
        upper,
        lower,
        staged=(incoming,),
    )
    upper, lower, incoming = extension(packed, head, tail)
    part, from_prev, from_next, returned = precondition(residual, upper, lower, incoming)
    return call(
        second_kernel,
        "assemble_second",
        field_t,
        [*lists, edges, tiles(rows), tiles(rows, F32), DMA((3,)), DMA((2,)), DMA((groups,))],
        cost(0, 10 * rows * tile),
        send_list,
        send_count,
        from_prev,
        from_next,
        first,
        staged=(part, returned),
    )


def solution(mesh):
    return jax.shard_map(
        per_device,
        mesh=mesh,
        in_specs=(
            P("slab", "cross", None, None, None),
            P("slab", "cross", None, None, None, None),
            P("slab", "cross", None, None),
            P("slab", "cross", None, None, None, None),
            P("slab", "cross", None, None),
            P("slab", "cross", None, None),
            P("slab", "cross", None),
        ),
        out_specs=P("slab", "cross", None, None, None),
        check_vma=False,
    )
```

```python
import functools

import jax
import jax.numpy as jnp
from jax import lax
from jax.experimental import pallas as pl
from jax.experimental.pallas import tpu as pltpu
from jax.sharding import PartitionSpec as P

OVL = 4
GROUP = 8
BF = jnp.bfloat16
F32 = jnp.float32
HBM = pl.BlockSpec(memory_space=pltpu.HBM)
VMEM = pl.BlockSpec(memory_space=pltpu.VMEM)
DMA = pltpu.SemaphoreType.DMA


def params():
    return pltpu.CompilerParams(vmem_limit_bytes=36 * 1024 * 1024)


def cost(flops, nbytes):
    return pl.CostEstimate(flops=flops, bytes_accessed=nbytes, transcendentals=0)


def start(source, target, sem):
    copy = pltpu.make_async_copy(source, target, sem)
    copy.start()
    return copy


def wait_all(copies):
    for copy in copies:
        copy.wait()


def slot_target(list_ref, count_ref, slot):
    slots = list_ref.shape[2]
    peer, turn = slot // slots, slot % slots
    return list_ref[0, 0, turn, peer], turn < count_ref[0, 0, peer]


def start_packing(field_ref, packed_ref, out_hbm, list_ref, count_ref, sems):
    slots = out_hbm.shape[1]
    peers = GROUP // slots
    copies = []
    for g in range(packed_ref.shape[0] // GROUP):
        for slot in range(g * GROUP, (g + 1) * GROUP):
            row, used = slot_target(list_ref, count_ref, slot)
            packed_ref[slot] = jnp.where(used, field_ref[row], jnp.zeros((), field_ref.dtype)).astype(BF)
        for peer in range(g * peers, (g + 1) * peers):
            copies.append(start(packed_ref.at[pl.ds(peer * slots, slots)], out_hbm.at[peer], sems.at[peer]))
    return copies


def start_lists(list_hbm, count_hbm, list_ref, count_ref, sems):
    return [start(list_hbm, list_ref, sems.at[0]), start(count_hbm, count_ref, sems.at[1])]


def pack_rhs_kernel(list_hbm, count_hbm, rhs_hbm, out_hbm, head_hbm, tail_hbm, list_ref, count_ref, packed_ref, field_ref, in_sem, out_sem, row_sem):
    lists = start_lists(list_hbm, count_hbm, list_ref, count_ref, in_sem)
    field = start(rhs_hbm.at[0, 0], field_ref, in_sem.at[2])
    rows = field_ref.shape[0]
    wait_all(lists)
    field.wait()
    copies = start_packing(field_ref, packed_ref, out_hbm, list_ref, count_ref, row_sem)
    copies.append(start(field_ref.at[pl.ds(0, OVL)], head_hbm, out_sem.at[0]))
    copies.append(start(field_ref.at[pl.ds(rows - OVL, OVL)], tail_hbm, out_sem.at[1]))
    wait_all(copies)


def start_blocks(blocks_hbm, first, chunk_ref, sems, order):
    copies = []
    for g in order:
        source = blocks_hbm.at[0, 0, pl.ds(first + g * GROUP, GROUP)]
        copies.append(start(source, chunk_ref.at[pl.ds(g * GROUP, GROUP)], sems.at[g]))
    return copies


def picked_product(chunk_ref, index, terms, picks, ext_ref):
    left = jnp.concatenate([chunk_ref[index, k] for k in terms], axis=1)
    right = jnp.concatenate([ext_ref[pick] for pick in picks], axis=0)
    return jnp.dot(left, right, preferred_element_type=F32)


def row_product(chunk_ref, index, cols_ref, row, ext_ref):
    terms = range(chunk_ref.shape[1])
    return picked_product(chunk_ref, index, terms, [cols_ref[0, k, 0, row] for k in terms], ext_ref)


def stage_kernel(own_hbm, upper_hbm, lower_hbm, blocks_hbm, near_ref, *refs):
    *chunk_refs, sems, block_sem = refs
    near = near_ref.shape[0]
    copies = start_near(own_hbm, upper_hbm, lower_hbm, near_ref, sems)
    for g, chunk_ref in enumerate(chunk_refs):
        copies.append(start(blocks_hbm.at[0, 0, pl.ds(near + g * GROUP, GROUP)], chunk_ref, block_sem.at[g]))
    wait_all(copies)


def half_row(low_ref, high_ref, row):
    half = low_ref.shape[0]
    return low_ref.at[row] if row < half else high_ref.at[row - half]


def near_residual_kernel(cols_hbm, blocks_hbm, rhs_hbm, own_hbm, upper_hbm, lower_hbm, low_ref, high_ref, cols_ref, ext_ref, chunk_ref, rhs_ref, in_sem, cols_sem, block_sem):
    rows = rhs_ref.shape[0]
    near = ext_ref.shape[0] - 1
    cols = start(cols_hbm, cols_ref, cols_sem.at[0])
    pieces = start_near(own_hbm, upper_hbm, lower_hbm, ext_ref, in_sem)
    pieces.append(start(rhs_hbm.at[0, 0], rhs_ref, in_sem.at[3]))
    groups = range(rows // GROUP)
    blocks = start_blocks(blocks_hbm, 0, chunk_ref, block_sem, groups)
    ext_ref[near] = jnp.zeros_like(ext_ref[near])
    cols.wait()
    wait_all(pieces)
    terms = chunk_ref.shape[1]
    for g, block in zip(groups, blocks):
        block.wait()
        for j in range(GROUP):
            i = g * GROUP + j
            picks = [jnp.minimum(cols_ref[0, k, 0, i], near) for k in range(terms)]
            half_row(low_ref, high_ref, i)[...] = rhs_ref[i].astype(F32) - picked_product(chunk_ref, i, range(terms), picks, ext_ref)


def fill_extended(near_ref, incoming_ref, ext_ref):
    near = near_ref.shape[0]
    ext_ref[:near] = near_ref[...]
    ext_ref[near:] = incoming_ref[...]


def margin_kernel(cols_hbm, blocks_hbm, near_ref, incoming_ref, *refs):
    *staged, cross_hbm, cols_ref, ext_ref, chunk_ref, part_ref, in_sem, block_sem, out_sem = refs
    cols = start(cols_hbm, cols_ref, in_sem.at[0])
    near = near_ref.shape[0]
    ready = len(staged)
    later = range(chunk_ref.shape[0] // GROUP)
    blocks = start_blocks(blocks_hbm, near + ready * GROUP, chunk_ref, block_sem, later)
    fill_extended(near_ref, incoming_ref, ext_ref)
    cols.wait()
    copies = []
    for g in range(ready + len(later)):
        if g >= ready:
            blocks[g - ready].wait()
        for j in range(GROUP):
            i = g * GROUP + j
            source, index = (staged[g], j) if g < ready else (chunk_ref, i - ready * GROUP)
            part_ref[i] = row_product(source, index, cols_ref, near + i, ext_ref).astype(BF)
        part = pl.ds(g * GROUP, GROUP)
        copies.append(start(part_ref.at[part], cross_hbm.at[part], out_sem.at[g]))
    wait_all(copies)


def start_near(own_hbm, upper_hbm, lower_hbm, ext_ref, sems):
    rows = own_hbm.shape[2]
    return [
        start(own_hbm.at[0, 0], ext_ref.at[pl.ds(0, rows)], sems.at[0]),
        start(upper_hbm, ext_ref.at[pl.ds(rows, OVL)], sems.at[1]),
        start(lower_hbm, ext_ref.at[pl.ds(rows + OVL, OVL)], sems.at[2]),
    ]


def own_kernel(cols_hbm, blocks_hbm, own_hbm, upper_hbm, lower_hbm, incoming_ref, part_ref, prev_hbm, next_hbm, cols_ref, ext_ref, chunk_ref, edge_ref, in_sem, cols_sem, block_sem, out_sem):
    rows = part_ref.shape[0]
    cols = start(cols_hbm, cols_ref, cols_sem.at[0])
    pieces = start_near(own_hbm, upper_hbm, lower_hbm, ext_ref, in_sem)
    last = rows // GROUP
    order = [last, *range(last)]
    blocks = start_blocks(blocks_hbm, 0, chunk_ref, block_sem, order)
    ext_ref[rows + 2 * OVL :] = incoming_ref[...]
    cols.wait()
    wait_all(pieces)
    copies = []
    for g, block in zip(order, blocks):
        block.wait()
        for j in range(GROUP):
            i = g * GROUP + j
            value = row_product(chunk_ref, i, cols_ref, i, ext_ref).astype(BF)
            if g == last:
                edge_ref[j] = value
            else:
                part_ref[i] = value
        if g == last:
            copies.append(start(edge_ref.at[pl.ds(0, OVL)], prev_hbm, out_sem.at[0]))
            copies.append(start(edge_ref.at[pl.ds(OVL, OVL)], next_hbm, out_sem.at[1]))
    wait_all(copies)


def add_returns(sum_ref, list_ref, count_ref, lists, edges, edge_ref, part_ref, returned_ref):
    rows = part_ref.shape[0]
    sum_ref[...] = part_ref[...].astype(F32)
    wait_all(lists)
    for slot in range(returned_ref.shape[0]):
        row, used = slot_target(list_ref, count_ref, slot)
        sum_ref[row] += jnp.where(used, returned_ref[slot].astype(F32), 0.0)

    wait_all(edges)
    sum_ref[:OVL] += edge_ref[0].astype(F32)
    sum_ref[rows - OVL :] += edge_ref[1].astype(F32)


def start_edges(from_prev_hbm, from_next_hbm, edge_ref, sems):
    return [start(from_prev_hbm, edge_ref.at[0], sems.at[0]), start(from_next_hbm, edge_ref.at[1], sems.at[1])]


def first_kernel(list_hbm, count_hbm, from_prev_hbm, from_next_hbm, part_ref, returned_ref, first_hbm, out_hbm, head_hbm, tail_hbm, list_ref, count_ref, edge_ref, packed_ref, field_ref, sum_ref, in_sem, edge_sem, out_sem, row_sem):
    lists = start_lists(list_hbm, count_hbm, list_ref, count_ref, in_sem)
    edges = start_edges(from_prev_hbm, from_next_hbm, edge_ref, edge_sem)
    add_returns(sum_ref, list_ref, count_ref, lists, edges, edge_ref, part_ref, returned_ref)
    rows = field_ref.shape[0]
    copies = start_packing(sum_ref, packed_ref, out_hbm, list_ref, count_ref, row_sem)
    field_ref[...] = sum_ref[...].astype(BF)
    copies.append(start(field_ref, first_hbm.at[0, 0], out_sem.at[2]))
    copies.append(start(field_ref.at[pl.ds(0, OVL)], head_hbm, out_sem.at[0]))
    copies.append(start(field_ref.at[pl.ds(rows - OVL, OVL)], tail_hbm, out_sem.at[1]))
    wait_all(copies)


def listed_residual_kernel(near, cols_hbm, list_hbm, count_hbm, blocks_hbm, low_ref, high_ref, incoming_ref, out_hbm, cols_ref, list_ref, count_ref, packed_ref, ext_ref, chunk_ref, res_ref, in_sem, cols_sem, block_sem, row_sem):
    cols = start(cols_hbm, cols_ref, cols_sem.at[0])
    groups = range(res_ref.shape[0] // GROUP)
    terms = chunk_ref.shape[1]
    blocks = []
    for g in groups:
        part = pl.ds(g * GROUP, GROUP)
        blocks.append(start(blocks_hbm.at[0, 0, part, pl.ds(1, terms)], chunk_ref.at[part], block_sem.at[g]))
    lists = start_lists(list_hbm, count_hbm, list_ref, count_ref, in_sem)
    listed = incoming_ref.shape[0]
    ext_ref[:listed] = incoming_ref[...]
    ext_ref[listed] = jnp.zeros_like(ext_ref[listed])
    cols.wait()
    for g, block in zip(groups, blocks):
        block.wait()
        for j in range(GROUP):
            i = g * GROUP + j
            named = [cols_ref[0, k + 1, 0, i] for k in range(terms)]
            picks = [jnp.where(col >= near, col - near, listed) for col in named]
            image = picked_product(chunk_ref, i, range(terms), picks, ext_ref)
            res_ref[i] = (half_row(low_ref, high_ref, i)[...] - image).astype(BF)
    wait_all(lists)
    wait_all(start_packing(res_ref, packed_ref, out_hbm, list_ref, count_ref, row_sem))


def own_residual_kernel(cols_hbm, blocks_hbm, rhs_hbm, own_hbm, upper_hbm, lower_hbm, incoming_ref, res_hbm, head_hbm, tail_hbm, cols_ref, ext_ref, chunk_ref, res_ref, in_sem, cols_sem, block_sem, out_sem):
    rows = res_ref.shape[0]
    cols = start(cols_hbm, cols_ref, cols_sem.at[0])
    pieces = start_near(own_hbm, upper_hbm, lower_hbm, ext_ref, in_sem)
    pieces.append(start(rhs_hbm.at[0, 0], res_ref, in_sem.at[3]))
    groups = range(rows // GROUP)
    blocks = start_blocks(blocks_hbm, 0, chunk_ref, block_sem, groups)
    ext_ref[rows + 2 * OVL :] = incoming_ref[...]
    cols.wait()
    wait_all(pieces)
    for g, block in zip(groups, blocks):
        block.wait()
        for j in range(GROUP):
            i = g * GROUP + j
            image = row_product(chunk_ref, i, cols_ref, i, ext_ref)
            res_ref[i] = (res_ref[i].astype(F32) - image).astype(BF)
    wait_all([
        start(res_ref.at[pl.ds(0, OVL)], head_hbm, out_sem.at[0]),
        start(res_ref.at[pl.ds(rows - OVL, OVL)], tail_hbm, out_sem.at[1]),
        start(res_ref, res_hbm.at[0, 0], out_sem.at[2]),
    ])


def second_kernel(list_hbm, count_hbm, from_prev_hbm, from_next_hbm, first_hbm, part_ref, returned_ref, second_hbm, list_ref, count_ref, edge_ref, field_ref, sum_ref, in_sem, edge_sem, out_sem):
    lists = start_lists(list_hbm, count_hbm, list_ref, count_ref, in_sem)
    edges = start_edges(from_prev_hbm, from_next_hbm, edge_ref, edge_sem)
    base = start(first_hbm.at[0, 0], field_ref, in_sem.at[2])
    add_returns(sum_ref, list_ref, count_ref, lists, edges, edge_ref, part_ref, returned_ref)
    base.wait()
    stores = []
    for g in range(field_ref.shape[0] // GROUP):
        part = pl.ds(g * GROUP, GROUP)
        field_ref[part] = (field_ref[part].astype(F32) + sum_ref[part]).astype(BF)
        stores.append(start(field_ref.at[part], second_hbm.at[0, 0, part], out_sem.at[g]))
    wait_all(stores)


def to_next(x):
    count = lax.axis_size("slab")
    return lax.ppermute(x, "slab", [(i, i + 1) for i in range(count - 1)])


def to_prev(x):
    count = lax.axis_size("slab")
    return lax.ppermute(x, "slab", [(i + 1, i) for i in range(count - 1)])


def route(buffer):
    return lax.all_to_all(buffer, "cross", split_axis=0, concat_axis=0, tiled=True)


def per_device(rhs, m_blocks, m_cols, j_blocks, j_cols, send_list, send_count):
    _, _, rows, block, vectors = rhs.shape
    peers, slots = send_list.shape[2:]
    listed = peers * slots
    extended_rows, terms = m_blocks.shape[2:4]
    near_rows = rows + 2 * OVL
    groups = rows // GROUP
    tile = block * vectors
    field_t = pltpu.HBM(rhs.shape, BF)
    packed_t = pltpu.HBM((peers, slots, block, vectors), BF)
    edge_t = pltpu.HBM((OVL, block, vectors), BF)
    listed_t = pltpu.HBM((listed, block, vectors), BF)

    m_cols = jnp.transpose(m_cols, (0, 3, 1, 2))
    j_cols = jnp.transpose(j_cols, (0, 3, 1, 2))
    send_list = jnp.transpose(send_list, (0, 1, 3, 2))

    def smem(x):
        return pltpu.SMEM(x.shape, jnp.int32)

    def tiles(count, dtype=BF):
        return pltpu.VMEM((count, block, vectors), dtype)

    def chunk(count):
        return pltpu.VMEM((count, terms, block, block), BF)

    lists = [smem(send_list), smem(send_count)]
    edges = pltpu.VMEM((2, OVL, block, vectors), BF)

    def call(kernel, name, out_shape, scratch, estimate, *operands, staged=()):
        placed = [pltpu.with_memory_space_constraint(x, pltpu.HBM) for x in operands]
        placed += [pltpu.with_memory_space_constraint(x, pltpu.VMEM) for x in staged]
        spec = lambda t: pl.BlockSpec(memory_space=t.memory_space)
        return pl.pallas_call(
            kernel,
            out_shape=out_shape,
            in_specs=[HBM] * len(operands) + [VMEM] * len(staged),
            out_specs=tuple(map(spec, out_shape)) if isinstance(out_shape, tuple) else spec(out_shape),
            scratch_shapes=scratch,
            compiler_params=params(),
            cost_estimate=estimate,
            name=name,
        )(*placed)

    packed, head, tail = call(
        pack_rhs_kernel,
        "pack_rhs",
        (packed_t, edge_t, edge_t),
        [*lists, tiles(listed), tiles(rows), DMA((3,)), DMA((2,)), DMA((peers,))],
        cost(0, 4 * rows * tile),
        send_list,
        send_count,
        rhs,
    )

    def extension(packed, head, tail):
        incoming = route(packed).reshape(listed, block, vectors)
        return to_next(tail), to_prev(head), incoming

    def precondition(field, upper, lower, incoming):
        groups = listed // GROUP
        ready = 1
        near, *chunks = call(
            stage_kernel,
            "stage_slots",
            (tiles(near_rows), *[chunk(GROUP)] * ready),
            [DMA((3,)), DMA((ready,))],
            cost(0, 4 * (near_rows + terms * ready * GROUP) * tile),
            field,
            upper,
            lower,
            m_blocks,
        )
        cross = call(
            margin_kernel,
            "slot_partial",
            listed_t,
            [smem(m_cols), tiles(extended_rows), chunk(listed - ready * GROUP), tiles(listed), DMA((1,)), DMA((groups - ready,)), DMA((groups,))],
            cost(2 * listed * terms * block * tile, 12 * extended_rows * tile),
            m_cols,
            m_blocks,
            staged=(near, incoming, *chunks),
        )
        returned = route(cross.reshape(peers, slots, block, vectors)).reshape(listed, block, vectors)
        groups = near_rows // GROUP
        part, to_p, to_n = call(
            own_kernel,
            "own_partial",
            (tiles(rows), edge_t, edge_t),
            [smem(m_cols), tiles(extended_rows), chunk(near_rows), tiles(2 * OVL), DMA((3,)), DMA((1,)), DMA((groups,)), DMA((2,))],
            cost(2 * near_rows * terms * block * tile, 12 * extended_rows * tile),
            m_cols,
            m_blocks,
            field,
            upper,
            lower,
            staged=(incoming,),
        )
        from_next = to_prev(to_p)
        from_prev = to_next(to_n)
        return part, from_prev, from_next, returned

    upper, lower, incoming = extension(packed, head, tail)
    part, from_prev, from_next, returned = precondition(rhs, upper, lower, incoming)
    first, packed, head, tail = call(
        first_kernel,
        "assemble_first",
        (field_t, packed_t, edge_t, edge_t),
        [*lists, edges, tiles(listed), tiles(rows), tiles(rows, F32), DMA((2,)), DMA((2,)), DMA((3,)), DMA((peers,))],
        cost(0, 10 * rows * tile),
        send_list,
        send_count,
        from_prev,
        from_next,
        staged=(part, returned),
    )
    upper, lower, incoming = extension(packed, head, tail)
    low, high = call(
        near_residual_kernel,
        "near_residual",
        (tiles(rows // 2, F32), tiles(rows // 2, F32)),
        [smem(j_cols), tiles(near_rows + 1), chunk(rows), tiles(rows), DMA((4,)), DMA((1,)), DMA((groups,))],
        cost(2 * rows * terms * block * tile, 4 * (near_rows + terms * rows) * tile),
        j_cols,
        j_blocks,
        rhs,
        first,
        upper,
        lower,
    )
    packed = call(
        functools.partial(listed_residual_kernel, near_rows),
        "listed_residual",
        packed_t,
        [smem(j_cols), *lists, tiles(listed), tiles(listed + 1), pltpu.VMEM((rows, terms - 1, block, block), BF), tiles(rows), DMA((2,)), DMA((1,)), DMA((groups,)), DMA((peers,))],
        cost(2 * rows * terms * block * tile, 12 * extended_rows * tile),
        j_cols,
        send_list,
        send_count,
        j_blocks,
        staged=(low, high, incoming),
    )
    residual, head, tail = call(
        own_residual_kernel,
        "own_residual",
        (field_t, edge_t, edge_t),
        [smem(j_cols), tiles(extended_rows), chunk(rows), tiles(rows), DMA((4,)), DMA((1,)), DMA((groups,)), DMA((3,))],
        cost(2 * rows * terms * block * tile, 12 * extended_rows * tile),
        j_cols,
        j_blocks,
        rhs,
        first,
        upper,
        lower,
        staged=(incoming,),
    )
    upper, lower, incoming = extension(packed, head, tail)
    part, from_prev, from_next, returned = precondition(residual, upper, lower, incoming)
    return call(
        second_kernel,
        "assemble_second",
        field_t,
        [*lists, edges, tiles(rows), tiles(rows, F32), DMA((3,)), DMA((2,)), DMA((groups,))],
        cost(0, 10 * rows * tile),
        send_list,
        send_count,
        from_prev,
        from_next,
        first,
        staged=(part, returned),
    )


def solution(mesh):
    return jax.shard_map(
        per_device,
        mesh=mesh,
        in_specs=(
            P("slab", "cross", None, None, None),
            P("slab", "cross", None, None, None, None),
            P("slab", "cross", None, None),
            P("slab", "cross", None, None, None, None),
            P("slab", "cross", None, None),
            P("slab", "cross", None, None),
            P("slab", "cross", None),
        ),
        out_specs=P("slab", "cross", None, None, None),
        check_vma=False,
    )
```

```python
import functools

import jax
import jax.numpy as jnp
from jax import lax
from jax.experimental import pallas as pl
from jax.experimental.pallas import tpu as pltpu
from jax.sharding import PartitionSpec as P

OVL = 4
GROUP = 8
BF = jnp.bfloat16
F32 = jnp.float32
HBM = pl.BlockSpec(memory_space=pltpu.HBM)
VMEM = pl.BlockSpec(memory_space=pltpu.VMEM)
DMA = pltpu.SemaphoreType.DMA


def params():
    return pltpu.CompilerParams(vmem_limit_bytes=36 * 1024 * 1024)


def cost(flops, nbytes):
    return pl.CostEstimate(flops=flops, bytes_accessed=nbytes, transcendentals=0)


def start(source, target, sem):
    copy = pltpu.make_async_copy(source, target, sem)
    copy.start()
    return copy


def wait_all(copies):
    for copy in copies:
        copy.wait()


def slot_target(list_ref, count_ref, slot):
    slots = list_ref.shape[2]
    peer, turn = slot // slots, slot % slots
    return list_ref[0, 0, turn, peer], turn < count_ref[0, 0, peer]


def start_packing(field_ref, packed_ref, out_hbm, list_ref, count_ref, sems):
    slots = out_hbm.shape[1]
    peers = GROUP // slots
    copies = []
    for g in range(packed_ref.shape[0] // GROUP):
        for slot in range(g * GROUP, (g + 1) * GROUP):
            row, used = slot_target(list_ref, count_ref, slot)
            packed_ref[slot] = jnp.where(used, field_ref[row], jnp.zeros((), field_ref.dtype)).astype(BF)
        for peer in range(g * peers, (g + 1) * peers):
            copies.append(start(packed_ref.at[pl.ds(peer * slots, slots)], out_hbm.at[peer], sems.at[peer]))
    return copies


def start_lists(list_hbm, count_hbm, list_ref, count_ref, sems):
    return [start(list_hbm, list_ref, sems.at[0]), start(count_hbm, count_ref, sems.at[1])]


def pack_rhs_kernel(list_hbm, count_hbm, rhs_hbm, out_hbm, head_hbm, tail_hbm, list_ref, count_ref, packed_ref, field_ref, in_sem, out_sem, row_sem):
    lists = start_lists(list_hbm, count_hbm, list_ref, count_ref, in_sem)
    field = start(rhs_hbm.at[0, 0], field_ref, in_sem.at[2])
    rows = field_ref.shape[0]
    wait_all(lists)
    field.wait()
    copies = start_packing(field_ref, packed_ref, out_hbm, list_ref, count_ref, row_sem)
    copies.append(start(field_ref.at[pl.ds(0, OVL)], head_hbm, out_sem.at[0]))
    copies.append(start(field_ref.at[pl.ds(rows - OVL, OVL)], tail_hbm, out_sem.at[1]))
    wait_all(copies)


def start_blocks(blocks_hbm, first, chunk_ref, sems, order):
    copies = []
    for g in order:
        source = blocks_hbm.at[0, 0, pl.ds(first + g * GROUP, GROUP)]
        copies.append(start(source, chunk_ref.at[pl.ds(g * GROUP, GROUP)], sems.at[g]))
    return copies


def picked_product(chunk_ref, index, terms, picks, ext_ref):
    left = jnp.concatenate([chunk_ref[index, k] for k in terms], axis=1)
    right = jnp.concatenate([ext_ref[pick] for pick in picks], axis=0)
    return jnp.dot(left, right, preferred_element_type=F32)


def row_product(chunk_ref, index, cols_ref, row, ext_ref):
    terms = range(chunk_ref.shape[1])
    return picked_product(chunk_ref, index, terms, [cols_ref[0, k, 0, row] for k in terms], ext_ref)


def stage_kernel(own_hbm, upper_hbm, lower_hbm, blocks_hbm, near_ref, *refs):
    *chunk_refs, sems, block_sem = refs
    near = near_ref.shape[0]
    copies = start_near(own_hbm, upper_hbm, lower_hbm, near_ref, sems)
    for g, chunk_ref in enumerate(chunk_refs):
        copies.append(start(blocks_hbm.at[0, 0, pl.ds(near + g * GROUP, GROUP)], chunk_ref, block_sem.at[g]))
    wait_all(copies)


def half_row(low_ref, high_ref, row):
    half = low_ref.shape[0]
    return low_ref.at[row] if row < half else high_ref.at[row - half]


def near_residual_kernel(cols_hbm, blocks_hbm, rhs_hbm, own_hbm, upper_hbm, lower_hbm, low_ref, high_ref, ready_ref, cols_ref, ext_ref, chunk_ref, rhs_ref, in_sem, cols_sem, ready_sem, block_sem):
    rows = rhs_ref.shape[0]
    near = ext_ref.shape[0] - 1
    cols = start(cols_hbm, cols_ref, cols_sem.at[0])
    pieces = start_near(own_hbm, upper_hbm, lower_hbm, ext_ref, in_sem)
    pieces.append(start(rhs_hbm.at[0, 0], rhs_ref, in_sem.at[3]))
    groups = range(rows // GROUP)
    blocks = start_blocks(blocks_hbm, 0, chunk_ref, block_sem, groups)
    ready = start(blocks_hbm.at[0, 0, pl.ds(0, GROUP), pl.ds(1, ready_ref.shape[1])], ready_ref, ready_sem.at[0])
    ext_ref[near] = jnp.zeros_like(ext_ref[near])
    cols.wait()
    wait_all(pieces)
    terms = chunk_ref.shape[1]
    for g, block in zip(groups, blocks):
        block.wait()
        for j in range(GROUP):
            i = g * GROUP + j
            picks = [jnp.minimum(cols_ref[0, k, 0, i], near) for k in range(terms)]
            half_row(low_ref, high_ref, i)[...] = rhs_ref[i].astype(F32) - picked_product(chunk_ref, i, range(terms), picks, ext_ref)
    ready.wait()


def fill_extended(near_ref, incoming_ref, ext_ref):
    near = near_ref.shape[0]
    ext_ref[:near] = near_ref[...]
    ext_ref[near:] = incoming_ref[...]


def margin_kernel(cols_hbm, blocks_hbm, near_ref, incoming_ref, *refs):
    *staged, cross_hbm, cols_ref, ext_ref, chunk_ref, part_ref, in_sem, block_sem, out_sem = refs
    cols = start(cols_hbm, cols_ref, in_sem.at[0])
    near = near_ref.shape[0]
    ready = len(staged)
    later = range(chunk_ref.shape[0] // GROUP)
    blocks = start_blocks(blocks_hbm, near + ready * GROUP, chunk_ref, block_sem, later)
    fill_extended(near_ref, incoming_ref, ext_ref)
    cols.wait()
    copies = []
    for g in range(ready + len(later)):
        if g >= ready:
            blocks[g - ready].wait()
        for j in range(GROUP):
            i = g * GROUP + j
            source, index = (staged[g], j) if g < ready else (chunk_ref, i - ready * GROUP)
            part_ref[i] = row_product(source, index, cols_ref, near + i, ext_ref).astype(BF)
        part = pl.ds(g * GROUP, GROUP)
        copies.append(start(part_ref.at[part], cross_hbm.at[part], out_sem.at[g]))
    wait_all(copies)


def start_near(own_hbm, upper_hbm, lower_hbm, ext_ref, sems):
    rows = own_hbm.shape[2]
    return [
        start(own_hbm.at[0, 0], ext_ref.at[pl.ds(0, rows)], sems.at[0]),
        start(upper_hbm, ext_ref.at[pl.ds(rows, OVL)], sems.at[1]),
        start(lower_hbm, ext_ref.at[pl.ds(rows + OVL, OVL)], sems.at[2]),
    ]


def own_kernel(cols_hbm, blocks_hbm, own_hbm, upper_hbm, lower_hbm, incoming_ref, part_ref, prev_hbm, next_hbm, cols_ref, ext_ref, chunk_ref, edge_ref, in_sem, cols_sem, block_sem, out_sem):
    rows = part_ref.shape[0]
    cols = start(cols_hbm, cols_ref, cols_sem.at[0])
    pieces = start_near(own_hbm, upper_hbm, lower_hbm, ext_ref, in_sem)
    last = rows // GROUP
    order = [last, *range(last)]
    blocks = start_blocks(blocks_hbm, 0, chunk_ref, block_sem, order)
    ext_ref[rows + 2 * OVL :] = incoming_ref[...]
    cols.wait()
    wait_all(pieces)
    copies = []
    for g, block in zip(order, blocks):
        block.wait()
        for j in range(GROUP):
            i = g * GROUP + j
            value = row_product(chunk_ref, i, cols_ref, i, ext_ref).astype(BF)
            if g == last:
                edge_ref[j] = value
            else:
                part_ref[i] = value
        if g == last:
            copies.append(start(edge_ref.at[pl.ds(0, OVL)], prev_hbm, out_sem.at[0]))
            copies.append(start(edge_ref.at[pl.ds(OVL, OVL)], next_hbm, out_sem.at[1]))
    wait_all(copies)


def add_returns(sum_ref, list_ref, count_ref, lists, edges, edge_ref, part_ref, returned_ref):
    rows = part_ref.shape[0]
    sum_ref[...] = part_ref[...].astype(F32)
    wait_all(lists)
    for slot in range(returned_ref.shape[0]):
        row, used = slot_target(list_ref, count_ref, slot)
        sum_ref[row] += jnp.where(used, returned_ref[slot].astype(F32), 0.0)

    wait_all(edges)
    sum_ref[:OVL] += edge_ref[0].astype(F32)
    sum_ref[rows - OVL :] += edge_ref[1].astype(F32)


def start_edges(from_prev_hbm, from_next_hbm, edge_ref, sems):
    return [start(from_prev_hbm, edge_ref.at[0], sems.at[0]), start(from_next_hbm, edge_ref.at[1], sems.at[1])]


def first_kernel(list_hbm, count_hbm, from_prev_hbm, from_next_hbm, part_ref, returned_ref, first_hbm, out_hbm, head_hbm, tail_hbm, list_ref, count_ref, edge_ref, packed_ref, field_ref, sum_ref, in_sem, edge_sem, out_sem, row_sem):
    lists = start_lists(list_hbm, count_hbm, list_ref, count_ref, in_sem)
    edges = start_edges(from_prev_hbm, from_next_hbm, edge_ref, edge_sem)
    add_returns(sum_ref, list_ref, count_ref, lists, edges, edge_ref, part_ref, returned_ref)
    rows = field_ref.shape[0]
    copies = start_packing(sum_ref, packed_ref, out_hbm, list_ref, count_ref, row_sem)
    field_ref[...] = sum_ref[...].astype(BF)
    copies.append(start(field_ref, first_hbm.at[0, 0], out_sem.at[2]))
    copies.append(start(field_ref.at[pl.ds(0, OVL)], head_hbm, out_sem.at[0]))
    copies.append(start(field_ref.at[pl.ds(rows - OVL, OVL)], tail_hbm, out_sem.at[1]))
    wait_all(copies)


def listed_residual_kernel(near, cols_hbm, list_hbm, count_hbm, blocks_hbm, low_ref, high_ref, ready_ref, incoming_ref, out_hbm, cols_ref, list_ref, count_ref, packed_ref, ext_ref, chunk_ref, res_ref, in_sem, cols_sem, block_sem, row_sem):
    cols = start(cols_hbm, cols_ref, cols_sem.at[0])
    groups = range(res_ref.shape[0] // GROUP)
    terms = chunk_ref.shape[1]
    blocks = [None]
    for g in groups[1:]:
        source = blocks_hbm.at[0, 0, pl.ds(g * GROUP, GROUP), pl.ds(1, terms)]
        blocks.append(start(source, chunk_ref.at[pl.ds((g - 1) * GROUP, GROUP)], block_sem.at[g - 1]))
    lists = start_lists(list_hbm, count_hbm, list_ref, count_ref, in_sem)
    listed = incoming_ref.shape[0]
    ext_ref[:listed] = incoming_ref[...]
    ext_ref[listed] = jnp.zeros_like(ext_ref[listed])
    cols.wait()
    for g, block in zip(groups, blocks):
        if g > 0:
            block.wait()
        for j in range(GROUP):
            i = g * GROUP + j
            named = [cols_ref[0, k + 1, 0, i] for k in range(terms)]
            picks = [jnp.where(col >= near, col - near, listed) for col in named]
            source, index = (chunk_ref, i - GROUP) if g > 0 else (ready_ref, j)
            image = picked_product(source, index, range(terms), picks, ext_ref)
            res_ref[i] = (half_row(low_ref, high_ref, i)[...] - image).astype(BF)
    wait_all(lists)
    wait_all(start_packing(res_ref, packed_ref, out_hbm, list_ref, count_ref, row_sem))


def own_residual_kernel(cols_hbm, blocks_hbm, rhs_hbm, own_hbm, upper_hbm, lower_hbm, incoming_ref, res_hbm, head_hbm, tail_hbm, cols_ref, ext_ref, chunk_ref, res_ref, in_sem, cols_sem, block_sem, out_sem):
    rows = res_ref.shape[0]
    cols = start(cols_hbm, cols_ref, cols_sem.at[0])
    pieces = start_near(own_hbm, upper_hbm, lower_hbm, ext_ref, in_sem)
    pieces.append(start(rhs_hbm.at[0, 0], res_ref, in_sem.at[3]))
    groups = range(rows // GROUP)
    blocks = start_blocks(blocks_hbm, 0, chunk_ref, block_sem, groups)
    ext_ref[rows + 2 * OVL :] = incoming_ref[...]
    cols.wait()
    wait_all(pieces)
    for g, block in zip(groups, blocks):
        block.wait()
        for j in range(GROUP):
            i = g * GROUP + j
            image = row_product(chunk_ref, i, cols_ref, i, ext_ref)
            res_ref[i] = (res_ref[i].astype(F32) - image).astype(BF)
    wait_all([
        start(res_ref.at[pl.ds(0, OVL)], head_hbm, out_sem.at[0]),
        start(res_ref.at[pl.ds(rows - OVL, OVL)], tail_hbm, out_sem.at[1]),
        start(res_ref, res_hbm.at[0, 0], out_sem.at[2]),
    ])


def second_kernel(list_hbm, count_hbm, from_prev_hbm, from_next_hbm, first_hbm, part_ref, returned_ref, second_hbm, list_ref, count_ref, edge_ref, field_ref, sum_ref, in_sem, edge_sem, out_sem):
    lists = start_lists(list_hbm, count_hbm, list_ref, count_ref, in_sem)
    edges = start_edges(from_prev_hbm, from_next_hbm, edge_ref, edge_sem)
    base = start(first_hbm.at[0, 0], field_ref, in_sem.at[2])
    add_returns(sum_ref, list_ref, count_ref, lists, edges, edge_ref, part_ref, returned_ref)
    base.wait()
    stores = []
    for g in range(field_ref.shape[0] // GROUP):
        part = pl.ds(g * GROUP, GROUP)
        field_ref[part] = (field_ref[part].astype(F32) + sum_ref[part]).astype(BF)
        stores.append(start(field_ref.at[part], second_hbm.at[0, 0, part], out_sem.at[g]))
    wait_all(stores)


def to_next(x):
    count = lax.axis_size("slab")
    return lax.ppermute(x, "slab", [(i, i + 1) for i in range(count - 1)])


def to_prev(x):
    count = lax.axis_size("slab")
    return lax.ppermute(x, "slab", [(i + 1, i) for i in range(count - 1)])


def route(buffer):
    return lax.all_to_all(buffer, "cross", split_axis=0, concat_axis=0, tiled=True)


def per_device(rhs, m_blocks, m_cols, j_blocks, j_cols, send_list, send_count):
    _, _, rows, block, vectors = rhs.shape
    peers, slots = send_list.shape[2:]
    listed = peers * slots
    extended_rows, terms = m_blocks.shape[2:4]
    near_rows = rows + 2 * OVL
    groups = rows // GROUP
    tile = block * vectors
    field_t = pltpu.HBM(rhs.shape, BF)
    packed_t = pltpu.HBM((peers, slots, block, vectors), BF)
    edge_t = pltpu.HBM((OVL, block, vectors), BF)
    listed_t = pltpu.HBM((listed, block, vectors), BF)

    m_cols = jnp.transpose(m_cols, (0, 3, 1, 2))
    j_cols = jnp.transpose(j_cols, (0, 3, 1, 2))
    send_list = jnp.transpose(send_list, (0, 1, 3, 2))

    def smem(x):
        return pltpu.SMEM(x.shape, jnp.int32)

    def tiles(count, dtype=BF):
        return pltpu.VMEM((count, block, vectors), dtype)

    def chunk(count):
        return pltpu.VMEM((count, terms, block, block), BF)

    def later_blocks(count):
        return pltpu.VMEM((count, terms - 1, block, block), BF)

    lists = [smem(send_list), smem(send_count)]
    edges = pltpu.VMEM((2, OVL, block, vectors), BF)

    def call(kernel, name, out_shape, scratch, estimate, *operands, staged=()):
        placed = [pltpu.with_memory_space_constraint(x, pltpu.HBM) for x in operands]
        placed += [pltpu.with_memory_space_constraint(x, pltpu.VMEM) for x in staged]
        spec = lambda t: pl.BlockSpec(memory_space=t.memory_space)
        return pl.pallas_call(
            kernel,
            out_shape=out_shape,
            in_specs=[HBM] * len(operands) + [VMEM] * len(staged),
            out_specs=tuple(map(spec, out_shape)) if isinstance(out_shape, tuple) else spec(out_shape),
            scratch_shapes=scratch,
            compiler_params=params(),
            cost_estimate=estimate,
            name=name,
        )(*placed)

    packed, head, tail = call(
        pack_rhs_kernel,
        "pack_rhs",
        (packed_t, edge_t, edge_t),
        [*lists, tiles(listed), tiles(rows), DMA((3,)), DMA((2,)), DMA((peers,))],
        cost(0, 4 * rows * tile),
        send_list,
        send_count,
        rhs,
    )

    def extension(packed, head, tail):
        incoming = route(packed).reshape(listed, block, vectors)
        return to_next(tail), to_prev(head), incoming

    def precondition(field, upper, lower, incoming):
        groups = listed // GROUP
        ready = 1
        near, *chunks = call(
            stage_kernel,
            "stage_slots",
            (tiles(near_rows), *[chunk(GROUP)] * ready),
            [DMA((3,)), DMA((ready,))],
            cost(0, 4 * (near_rows + terms * ready * GROUP) * tile),
            field,
            upper,
            lower,
            m_blocks,
        )
        cross = call(
            margin_kernel,
            "slot_partial",
            listed_t,
            [smem(m_cols), tiles(extended_rows), chunk(listed - ready * GROUP), tiles(listed), DMA((1,)), DMA((groups - ready,)), DMA((groups,))],
            cost(2 * listed * terms * block * tile, 12 * extended_rows * tile),
            m_cols,
            m_blocks,
            staged=(near, incoming, *chunks),
        )
        returned = route(cross.reshape(peers, slots, block, vectors)).reshape(listed, block, vectors)
        groups = near_rows // GROUP
        part, to_p, to_n = call(
            own_kernel,
            "own_partial",
            (tiles(rows), edge_t, edge_t),
            [smem(m_cols), tiles(extended_rows), chunk(near_rows), tiles(2 * OVL), DMA((3,)), DMA((1,)), DMA((groups,)), DMA((2,))],
            cost(2 * near_rows * terms * block * tile, 12 * extended_rows * tile),
            m_cols,
            m_blocks,
            field,
            upper,
            lower,
            staged=(incoming,),
        )
        from_next = to_prev(to_p)
        from_prev = to_next(to_n)
        return part, from_prev, from_next, returned

    upper, lower, incoming = extension(packed, head, tail)
    part, from_prev, from_next, returned = precondition(rhs, upper, lower, incoming)
    first, packed, head, tail = call(
        first_kernel,
        "assemble_first",
        (field_t, packed_t, edge_t, edge_t),
        [*lists, edges, tiles(listed), tiles(rows), tiles(rows, F32), DMA((2,)), DMA((2,)), DMA((3,)), DMA((peers,))],
        cost(0, 10 * rows * tile),
        send_list,
        send_count,
        from_prev,
        from_next,
        staged=(part, returned),
    )
    upper, lower, incoming = extension(packed, head, tail)
    low, high, ready = call(
        near_residual_kernel,
        "near_residual",
        (tiles(rows // 2, F32), tiles(rows // 2, F32), later_blocks(GROUP)),
        [smem(j_cols), tiles(near_rows + 1), chunk(rows), tiles(rows), DMA((4,)), DMA((1,)), DMA((1,)), DMA((groups,))],
        cost(2 * rows * terms * block * tile, 4 * (near_rows + terms * rows) * tile),
        j_cols,
        j_blocks,
        rhs,
        first,
        upper,
        lower,
    )
    packed = call(
        functools.partial(listed_residual_kernel, near_rows),
        "listed_residual",
        packed_t,
        [smem(j_cols), *lists, tiles(listed), tiles(listed + 1), later_blocks(rows - GROUP), tiles(rows), DMA((2,)), DMA((1,)), DMA((groups - 1,)), DMA((peers,))],
        cost(2 * rows * terms * block * tile, 12 * extended_rows * tile),
        j_cols,
        send_list,
        send_count,
        j_blocks,
        staged=(low, high, ready, incoming),
    )
    residual, head, tail = call(
        own_residual_kernel,
        "own_residual",
        (field_t, edge_t, edge_t),
        [smem(j_cols), tiles(extended_rows), chunk(rows), tiles(rows), DMA((4,)), DMA((1,)), DMA((groups,)), DMA((3,))],
        cost(2 * rows * terms * block * tile, 12 * extended_rows * tile),
        j_cols,
        j_blocks,
        rhs,
        first,
        upper,
        lower,
        staged=(incoming,),
    )
    upper, lower, incoming = extension(packed, head, tail)
    part, from_prev, from_next, returned = precondition(residual, upper, lower, incoming)
    return call(
        second_kernel,
        "assemble_second",
        field_t,
        [*lists, edges, tiles(rows), tiles(rows, F32), DMA((3,)), DMA((2,)), DMA((groups,))],
        cost(0, 10 * rows * tile),
        send_list,
        send_count,
        from_prev,
        from_next,
        first,
        staged=(part, returned),
    )


def solution(mesh):
    return jax.shard_map(
        per_device,
        mesh=mesh,
        in_specs=(
            P("slab", "cross", None, None, None),
            P("slab", "cross", None, None, None, None),
            P("slab", "cross", None, None),
            P("slab", "cross", None, None, None, None),
            P("slab", "cross", None, None),
            P("slab", "cross", None, None),
            P("slab", "cross", None),
        ),
        out_specs=P("slab", "cross", None, None, None),
        check_vma=False,
    )
```
